256 devices in a mesh: region: 64 (over y_hi, x, z), mp: 4 (over y_lo, core).
Axes of the slice: x: 4, y: 4 (y_hi: 2, y_lo: 2; y = y_hi * 2 + y_lo), z: 8, core: 2. Of those that a mesh axis runs over, the one named last changes fastest.
Arguments:
- tile_data: bfloat16 [256, 256, 2048], P('region', None, 'mp'), may hold values from -6.5 to 6.5
- tile_counts: int32 [64], replicated, may hold values from 0 to 4, as said below
- modulation: bfloat16 [64, 3, 2048], P('region'), may hold values from -4 to 4
- qkv_weight: bfloat16 [2048, 3, 2048], P('region', None, 'mp'), may hold values from -0.92807765 to 0.92807765
- out_weight: bfloat16 [2048, 2048], P('region', 'mp'), may hold values from -0.125 to 0.125
- blend_weights: float32 [6], replicated, may hold values from 0.1 to 0.9
Outputs:
- blended: bfloat16 [256, 256, 2048], P('region', None, 'mp')
The draws below stay inside these ranges and needn't reach their ends.
Inputs may be any that keep to these rules, and one draw needn't show every extreme that they name: `tile_counts`: groups 2m and 2m + 1 together hold exactly 4 tiles. In every draw some group holds 4 tiles and its partner none.
All inputs are finite; a program needn't handle non-finite values.
Results may differ from the reference program's by a relative error of at most 0.0071.
Values may be sent and summed in bfloat16 or wider, within the bound.
No kernel may reach another device: no remote copies, remote signals or barrier semaphores. Data moves between devices by JAX's collectives and lax.ppermute only.
A program may use at most 64 MiB of HBM per device.

```python
import math
import jax
import jax.numpy as jnp
from jax import lax

D = 2048
HEADS = 16
HDIM = 128
S = 16
TOK = 256
W = 6
TCOLS = 8
TPD = 2
PAIRT = 4
GROUPS = 64


def draw_tile_data(key, part):
    key = jax.random.fold_in(key, 11)
    normal_part = jnp.clip(jax.random.normal(key, (GROUPS * PAIRT, TOK, D), jnp.float32), -6.0, 6.0)
    return normal_part.astype(jnp.bfloat16)


def draw_tile_counts(key, part):
    key = jax.random.fold_in(key, 37)
    pair_total = GROUPS // 2
    even_counts = jax.random.randint(key, (pair_total,), 0, PAIRT + 1)
    chosen = jax.random.randint(jax.random.fold_in(key, 1), (), 0, pair_total)
    extreme = jax.random.randint(jax.random.fold_in(key, 2), (), 0, 2) * PAIRT
    even_counts = jnp.where(jnp.arange(pair_total) == chosen, extreme, even_counts)
    return jnp.stack([even_counts, PAIRT - even_counts], axis=1).reshape(GROUPS).astype(jnp.int32)


def draw_qkv_weight(key, part):
    key = jax.random.fold_in(key, 23)
    normal_part = jnp.clip(jax.random.normal(key, (D, 3, D), jnp.float32), -4.0, 4.0)
    return (normal_part / math.sqrt(D)).astype(jnp.bfloat16)


def level_of(own_key, dims, shards, smallest, largest):
    gain = 1.0
    for axis_at, blocks in shards:
        draws = jax.random.uniform(jax.random.fold_in(jax.random.fold_in(own_key, 6), axis_at), (blocks,), jnp.float32, smallest / len(shards), largest / len(shards))
        gain = gain * jnp.repeat(jnp.exp(draws), dims[axis_at] // blocks).reshape((-1,) + (1,) * (len(dims) - 1 - axis_at))
    return gain


def scatter_about(rng, dims, width, limit, shards=(), kind=jnp.bfloat16):
    array = width * jax.random.normal(rng, dims, jnp.float32)
    if shards:
        array = array * level_of(rng, dims, shards, -0.22, 0.18)
    return jnp.clip(array, -limit, limit).astype(kind)


def setup_inputs(seed: int = 0) -> dict:
    key_list = jax.random.split(jax.random.key(seed), 7)
    return {
        "tile_data": draw_tile_data(jax.random.fold_in(key_list[6], 71), 0),
        "tile_counts": draw_tile_counts(jax.random.fold_in(key_list[6], 71), 0),
        "modulation": scatter_about(key_list[2], (GROUPS, 3, D), 1.0, 4.0, ((0, 64),)),
        "qkv_weight": draw_qkv_weight(jax.random.fold_in(key_list[6], 71), 0),
        "out_weight": scatter_about(key_list[4], (D, D), D ** -0.5, 0.125, ((0, 64), (1, 4))),
        "blend_weights": jnp.clip(jax.random.uniform(key_list[5], (W,), jnp.float32, 0.1, 0.9), 0.1, 0.9),
    }


def normalise(values):
    row_mean = lax.optimization_barrier(jnp.mean(values, axis=-1, keepdims=True))
    centred = values - row_mean
    spread = lax.optimization_barrier(jnp.mean(centred * centred, axis=-1, keepdims=True))
    return centred * lax.rsqrt(spread + 1e-06)

def one_tile(tile_rows, modulators, qkv_weight, out_weight):
    values = tile_rows.astype(jnp.float32)
    mod_values = modulators.astype(jnp.float32)
    hidden = (normalise(values) * (1.0 + mod_values[1]) + mod_values[0]).astype(jnp.bfloat16)
    projections = jnp.dot(hidden, qkv_weight.reshape(D, 3 * D), preferred_element_type=jnp.float32)
    projections = lax.optimization_barrier(projections.astype(jnp.bfloat16))
    projections = projections.astype(jnp.float32).reshape(TOK, 3, HEADS, HDIM)
    scores = jnp.einsum('qhe,khe->hqk', projections[:, 0], projections[:, 1]) / math.sqrt(HDIM)
    attention_weights = lax.optimization_barrier(jax.nn.softmax(scores, axis=-1).astype(jnp.bfloat16))
    attended = jnp.einsum('hqk,khe->qhe', attention_weights.astype(jnp.float32), projections[:, 2])
    attended = attended.astype(jnp.bfloat16).reshape(TOK, D)
    projected = jnp.dot(attended, out_weight.T, preferred_element_type=jnp.float32)
    return (values + mod_values[2] * projected).astype(jnp.bfloat16)

def reference(tile_data, tile_counts, modulation, qkv_weight, out_weight, blend_weights):
    tile_total = TPD * tile_counts.shape[0]
    group_ends = jnp.cumsum(tile_counts).astype(jnp.int32)
    group_starts = (group_ends - tile_counts).astype(jnp.int32)
    tile_ids = jnp.arange(tile_total, dtype=jnp.int32)
    owner_ids = lax.optimization_barrier(jnp.sum((group_ends[None, :] <= tile_ids[:, None]).astype(jnp.int32), axis=1)).astype(jnp.int32)
    slot_ids = (tile_ids - group_starts[owner_ids]).astype(jnp.int32)
    slot_rows = (owner_ids * PAIRT + slot_ids).astype(jnp.int32)

    def process(carried):
        return one_tile(tile_data[carried[0]], modulation[carried[1]], qkv_weight, out_weight)
    updated = lax.map(process, (slot_rows, owner_ids))
    tile_grid = updated.reshape(tile_total // TCOLS, TCOLS, S, S, D).astype(jnp.float32)
    shares = blend_weights.astype(jnp.float32)
    across = shares[None, None, None, :, None]
    mixture = (1.0 - across) * tile_grid[:, :-1, :, S - W:, :] + across * tile_grid[:, 1:, :, :W, :]
    joined = tile_grid.at[:, :-1, :, S - W:, :].set(mixture).at[:, 1:, :, :W, :].set(mixture)
    joined = lax.optimization_barrier(joined.astype(jnp.bfloat16)).astype(jnp.float32)
    downward = shares[None, None, :, None, None]
    mixture = (1.0 - downward) * joined[:-1, :, S - W:, :, :] + downward * joined[1:, :, :W, :, :]
    finished = joined.at[:-1, :, S - W:, :, :].set(mixture).at[1:, :, :W, :, :].set(mixture)
    finished = finished.astype(jnp.bfloat16).reshape(tile_total, TOK, D)
    output = jnp.zeros(tile_data.shape, jnp.bfloat16).at[slot_rows].set(finished)
    return output
```

```python
import functools
import math

import jax
import jax.numpy as jnp
from jax import lax
from jax.experimental import pallas as pl
from jax.experimental.pallas import tpu as pltpu
from jax.sharding import Mesh, PartitionSpec as P

D = 2048
HDIM = 128
S = 16
W = 6
TOK = 256
NARROW = 512
HALF = 256
REGION = ("h", "x", "z")
MP = ("yl", "c")
BF = jnp.bfloat16
F32 = jnp.float32


def xor_swap(block, axis, bit):
    size = lax.axis_size(axis)
    return lax.ppermute(block, axis, [(i, i ^ bit) for i in range(size)])


def shift(block, distance, allowed):
    route = [(i, i + distance) for i in range(64) if 0 <= i + distance < 64 and allowed(i)]
    return lax.ppermute(block, REGION, route)


def ring_of_four(block, axis, split_axis):
    near = xor_swap(block, axis, 1)
    side = xor_swap(block, axis, 3)
    half = block.shape[split_axis] // 2
    size = block.shape[split_axis]
    first = xor_swap(lax.slice_in_dim(side, 0, half, axis=split_axis), axis, 1)
    second = xor_swap(lax.slice_in_dim(near, half, size, axis=split_axis), axis, 3)
    return block, near, (first, second), side


def hidden_kernel(a_ref, b_ref, c_ref, d_ref, mod_ref, out_ref):
    parts = [r[...].astype(F32) for r in (a_ref, b_ref, c_ref, d_ref)]
    mean = sum(jnp.sum(p, axis=-1, keepdims=True) for p in parts) * (1.0 / D)
    parts = [p - mean for p in parts]
    spread = sum(jnp.sum(p * p, axis=-1, keepdims=True) for p in parts) * (1.0 / D)
    scale = lax.rsqrt(spread + 1e-06)
    mods = mod_ref[0].astype(F32)
    for j, p in enumerate(parts):
        cols = slice(j * NARROW, (j + 1) * NARROW)
        value = p * scale * (1.0 + mods[1:2, cols]) + mods[0:1, cols]
        out_ref[:, cols] = value.astype(BF)


def hidden_of(pieces, mods):
    rows = 128
    piece = pl.BlockSpec((rows, NARROW), lambda i: (i, 0))
    return pl.pallas_call(
        hidden_kernel,
        grid=(512 // rows,),
        in_specs=[piece] * 4 + [pl.BlockSpec((1, 3, D), lambda i: (i * rows // TOK, 0, 0))],
        out_specs=pl.BlockSpec((rows, D), lambda i: (i, 0)),
        out_shape=jax.ShapeDtypeStruct((512, D), BF),
        cost_estimate=pl.CostEstimate(flops=8 * 512 * D, bytes_accessed=4 * 512 * D, transcendentals=512),
        name="hidden",
    )(*pieces, mods)


def attend_kernel(slot_ref, hid_ref, qk_ref, v0, v1, v2, v3, out_ref, w_ref, sem):
    copies = []
    for hr in range(2):
        for xr in range(4):
            slot = slot_ref[hr * 4 + xr]
            copies.append(
                pltpu.make_async_copy(
                    qk_ref.at[:, xr, hr], w_ref.at[slot, :, :, pl.ds(0, 2 * HALF)], sem
                )
            )
            copies.append(
                pltpu.make_async_copy(
                    (v0, v1, v2, v3)[xr].at[:, hr],
                    w_ref.at[slot, :, :, pl.ds(2 * HALF, HALF)],
                    sem,
                )
            )
    for copy in copies:
        copy.start()
    for copy in copies:
        copy.wait()
    weight = w_ref[...].reshape(D, 3 * HALF)
    for t in range(2):
        rows = slice(t * TOK, (t + 1) * TOK)
        proj = jnp.dot(hid_ref[rows, :], weight, preferred_element_type=F32).astype(BF)
        for n in range(2):
            q = proj[:, n * HDIM : (n + 1) * HDIM]
            k = proj[:, HALF + n * HDIM : HALF + (n + 1) * HDIM]
            v = proj[:, 2 * HALF + n * HDIM : 2 * HALF + (n + 1) * HDIM]
            scores = lax.dot_general(
                q, k, (((1,), (1,)), ((), ())), preferred_element_type=F32
            ) * (1.0 / math.sqrt(HDIM))
            top = jnp.max(scores, axis=-1, keepdims=True)
            e = jnp.exp(scores - top)
            probs = (e / jnp.sum(e, axis=-1, keepdims=True)).astype(BF)
            got = jnp.dot(probs, v, preferred_element_type=F32)
            out_ref[rows, n * HDIM : (n + 1) * HDIM] = got.astype(BF)


def attended_of(slots, hidden, qk, vs):
    anywhere = pl.BlockSpec(memory_space=pl.ANY)
    vmem = pl.BlockSpec(memory_space=pltpu.VMEM)
    return pl.pallas_call(
        attend_kernel,
        in_specs=[pl.BlockSpec(memory_space=pltpu.SMEM), vmem] + [anywhere] * 5,
        out_specs=vmem,
        out_shape=jax.ShapeDtypeStruct((512, HALF), BF),
        scratch_shapes=[pltpu.VMEM((8, 8, 32, 3 * HALF), BF), pltpu.SemaphoreType.DMA],
        compiler_params=pltpu.CompilerParams(vmem_limit_bytes=32 * 2**20),
        cost_estimate=pl.CostEstimate(
            flops=2 * 512 * D * 768 + 4 * 4 * TOK * TOK * HDIM,
            bytes_accessed=6 * 2**20,
            transcendentals=4 * TOK * TOK,
        ),
        name="attend",
    )(slots, hidden, qk, *vs)


def project_kernel(slot_ref, own_ref, other_ref, o0, o1, o2, o3, keep_ref, send_ref, w_ref, sem):
    copies = []
    for xr in range(4):
        copies.append(
            pltpu.make_async_copy(
                (o0, o1, o2, o3)[xr].at[:, slot_ref[0]], w_ref.at[slot_ref[1 + xr]], sem
            )
        )
    for copy in copies:
        copy.start()
    for copy in copies:
        copy.wait()
    for b, out_ref in ((1, send_ref), (0, keep_ref)):
        weight = w_ref[2 * b : 2 * b + 2].reshape(NARROW, NARROW)
        total = lax.dot_general(
            own_ref[...], weight[:, :HALF], (((1,), (1,)), ((), ())), preferred_element_type=F32
        ) + lax.dot_general(
            other_ref[...], weight[:, HALF:], (((1,), (1,)), ((), ())), preferred_element_type=F32
        )
        out_ref[...] = total.astype(BF)


def partial_of(slots, own, other, os):
    anywhere = pl.BlockSpec(memory_space=pl.ANY)
    vmem = pl.BlockSpec(memory_space=pltpu.VMEM)
    return pl.pallas_call(
        project_kernel,
        in_specs=[pl.BlockSpec(memory_space=pltpu.SMEM), vmem, vmem] + [anywhere] * 4,
        out_specs=[vmem, vmem],
        out_shape=[jax.ShapeDtypeStruct((512, NARROW), BF)] * 2,
        scratch_shapes=[pltpu.VMEM((4, 8, 32, NARROW), BF), pltpu.SemaphoreType.DMA],
        compiler_params=pltpu.CompilerParams(vmem_limit_bytes=32 * 2**20),
        cost_estimate=pl.CostEstimate(
            flops=2 * 512 * 512 * 1024, bytes_accessed=3 * 2**20, transcendentals=0
        ),
        name="project",
    )(slots, own, other, *os)


def mix(earlier, later, share):
    return (1.0 - share) * earlier.astype(F32) + share * later.astype(F32)


def join_columns(grid, region, shares):
    share = shares.reshape(1, W, 1)
    west, east = grid[:, :, :W], grid[:, :, S - W :]
    later = shift(west[0], -1, lambda i: i % 4 != 0)
    earlier = shift(east[1], 1, lambda i: i % 4 != 3)
    place = region % 4
    inner = mix(east[0], west[1], share).astype(BF)
    left = jnp.where(place != 0, mix(earlier, west[0], share).astype(BF), west[0])
    right = jnp.where(place != 3, mix(east[1], later, share).astype(BF), east[1])
    middle = grid[:, :, W : S - W]
    first = jnp.concatenate([left, middle[0], inner], axis=1)
    second = jnp.concatenate([inner, middle[1], right], axis=1)
    return jnp.stack([first, second])


def join_rows(grid, region, shares):
    share = shares.reshape(1, W, 1, 1)
    north, south = grid[:, :W], grid[:, S - W :]
    later = shift(north, -4, lambda i: True)
    earlier = shift(south, 4, lambda i: True)
    top = jnp.where(region >= 4, mix(earlier, north, share).astype(BF), north)
    bottom = jnp.where(region < 60, mix(south, later, share).astype(BF), south)
    return jnp.concatenate([top, grid[:, W : S - W], bottom], axis=1)


def pick(choices, index):
    return lax.dynamic_index_in_dim(choices, index, 0, keepdims=False)


def on_device(tile_data, tile_counts, modulation, qkv_weight, out_weight, blend_weights):
    h, x, z = (lax.axis_index(a) for a in REGION)
    yl, c = (lax.axis_index(a) for a in MP)
    region = h * 32 + x * 8 + z
    parity = z % 2
    even = jnp.sum(jnp.where(jnp.arange(64) == region - parity, tile_counts, 0))

    own_heads = jnp.where(h == 0, qkv_weight[:, :, :HALF], qkv_weight[:, :, HALF:])
    other_heads = jnp.where(h == 0, qkv_weight[:, :, HALF:], qkv_weight[:, :, :HALF])
    out_cols = jnp.where(
        h == 0, out_weight, jnp.concatenate([out_weight[:, HALF:], out_weight[:, :HALF]], axis=1)
    )
    out_swapped = jnp.concatenate([out_cols[:, HALF:], out_cols[:, :HALF]], axis=1)
    own_block = jnp.concatenate([own_heads.reshape(32, 3 * HALF), out_cols], axis=1)
    sent_block = jnp.concatenate([other_heads.reshape(32, 3 * HALF), out_swapped], axis=1)
    block = jnp.stack([own_block, xor_swap(sent_block, "h", 1)])
    qk_block, vo_block = block[:, :, : 2 * HALF], block[:, :, 2 * HALF :]

    vo_z = lax.all_gather(vo_block, "z", axis=0)
    p0, p1, p2, p3 = ring_of_four(qk_block, "x", 0)
    qk_x = jnp.stack([p0, p1, jnp.concatenate(p2, axis=0), p3])
    qk_all = lax.all_gather(qk_x, "z", axis=0)
    v_x = ring_of_four(vo_z[..., :HALF], "x", 0)
    o_x = ring_of_four(vo_z[..., HALF:], "x", 0)
    v_all = [v_x[0], v_x[1], jnp.concatenate(v_x[2], axis=0), v_x[3]]
    o_all = [o_x[0], o_x[1], jnp.concatenate(o_x[2], axis=0), o_x[3]]

    slots = jnp.arange(2)
    send_slot = jnp.where(parity == 0, 2 + slots, jnp.clip(slots - even, 0, 3))
    keep_slot = jnp.where(parity == 0, slots, jnp.clip(2 + slots - even, 0, 3))
    use_other = jnp.where(parity == 0, slots >= even, 2 + slots < even)
    sent = jnp.stack([pick(tile_data, send_slot[0]), pick(tile_data, send_slot[1])])
    kept = jnp.stack([pick(tile_data, keep_slot[0]), pick(tile_data, keep_slot[1])])
    came = xor_swap(sent, "z", 1)
    other_mod = xor_swap(modulation, "z", 1)
    tiles = jnp.where(use_other[:, None, None], came, kept)
    mods = jnp.where(use_other[:, None, None], other_mod, modulation)

    mine = tiles.reshape(512, NARROW)
    near = lax.ppermute(mine, ("h", "yl"), [(i, i ^ 1) for i in range(4)])
    side = lax.ppermute(mine, ("h", "yl"), [(i, i ^ 3) for i in range(4)])
    across_a = lax.ppermute(side[:HALF], ("h", "yl"), [(i, i ^ 1) for i in range(4)])
    across_b = lax.ppermute(near[HALF:], ("h", "yl"), [(i, i ^ 3) for i in range(4)])
    across = jnp.concatenate([across_a, across_b], axis=0)
    mods_across = xor_swap(mods, "h", 1)

    def in_order(m):
        m = m.reshape(2, 3, 2, 2, NARROW)
        m = jnp.where(yl == 0, m, m[:, :, ::-1])
        m = jnp.where(c == 0, m, m[:, :, :, ::-1])
        return m.reshape(2, 3, D)

    hid_own = hidden_of(
        (mine, xor_swap(mine, "c", 1), near, xor_swap(near, "c", 1)), in_order(mods)
    )
    hid_other = hidden_of(
        (across, xor_swap(across, "c", 1), side, xor_swap(side, "c", 1)), in_order(mods_across)
    )

    hr = jnp.arange(8) // 4
    place_x = (jnp.arange(8) % 4) ^ x
    place = ((hr ^ h) ^ yl) * 4 + ((place_x // 2) ^ c) * 2 + place_x % 2
    place = place.astype(jnp.int32)
    att_sent = attended_of(place, hid_other, qk_all, v_all)
    att_other = xor_swap(att_sent, "h", 1)
    att_own = attended_of(place, hid_own, qk_all, v_all)

    x_slots = place[:4] % 4
    sums = []
    for a in (1, 0):
        rows = jnp.concatenate([((yl ^ a) ^ h)[None], x_slots]).astype(jnp.int32)
        keep, send = partial_of(rows, att_own, att_other, o_all)
        sums.append((keep, xor_swap(send, "c", 1)))
    far = (sums[0][0].astype(F32) + sums[0][1].astype(F32)).astype(BF)
    far = xor_swap(far, "yl", 1)
    gate = mods[:, 2].reshape(2, 4, NARROW)
    gate = lax.dynamic_index_in_dim(gate, yl * 2 + c, 1, keepdims=True).astype(F32)
    summed = sums[1][0].astype(F32) + sums[1][1].astype(F32) + far.astype(F32)
    updated = tiles.astype(F32) + gate * summed.reshape(2, TOK, NARROW)
    grid = updated.astype(BF).reshape(2, S, S, NARROW)

    joined = join_columns(grid, region, blend_weights)
    finished = join_rows(joined, region, blend_weights).reshape(2, TOK, NARROW)

    other = xor_swap(finished, "z", 1)
    both = jnp.where(
        parity == 0,
        jnp.concatenate([finished, other], axis=0),
        jnp.concatenate([other, finished], axis=0),
    )
    outs = []
    for slot in range(4):
        source = jnp.where(parity == 0, slot, slot + even)
        live = jnp.where(parity == 0, slot < even, slot + even < 4)
        outs.append(jnp.where(live, pick(both, jnp.clip(source, 0, 3)), jnp.zeros((), BF)))
    return jnp.stack(outs)


def solution(mesh):
    fine = Mesh(mesh.devices.reshape(2, 4, 8, 2, 2), REGION + MP)
    return jax.shard_map(
        on_device,
        mesh=fine,
        in_specs=(
            P(REGION, None, MP),
            P(),
            P(REGION, None, None),
            P(REGION, None, MP),
            P(REGION, MP),
            P(),
        ),
        out_specs=P(REGION, None, MP),
        check_vma=False,
    )
```

```python
import functools
import math

import jax
import jax.numpy as jnp
from jax import lax
from jax.experimental import pallas as pl
from jax.experimental.pallas import tpu as pltpu
from jax.sharding import Mesh, PartitionSpec as P

D = 2048
HDIM = 128
S = 16
W = 6
TOK = 256
NARROW = 512
HALF = 256
REGION = ("h", "x", "z")
MP = ("yl", "c")
BF = jnp.bfloat16
F32 = jnp.float32


def xor_swap(block, axis, bit):
    size = math.prod(lax.axis_size(a) for a in ((axis,) if isinstance(axis, str) else axis))
    return lax.ppermute(block, axis, [(i, i ^ bit) for i in range(size)])


def rotate(block, axis, step):
    size = lax.axis_size(axis)
    return lax.ppermute(block, axis, [(i, (i + step) % size) for i in range(size)])


def shift(block, distance, allowed):
    route = [(i, i + distance) for i in range(64) if 0 <= i + distance < 64 and allowed(i)]
    return lax.ppermute(block, REGION, route)


def opposite(near, side, axis, split_axis):
    size = near.shape[split_axis]
    first = xor_swap(lax.slice_in_dim(side, 0, size // 2, axis=split_axis), axis, 1)
    second = xor_swap(lax.slice_in_dim(near, size // 2, size, axis=split_axis), axis, 3)
    return jnp.concatenate([first, second], axis=split_axis)


def ring_of_four(block, axis, split_axis):
    near = xor_swap(block, axis, 1)
    side = xor_swap(block, axis, 3)
    return block, near, opposite(near, side, axis, split_axis), side


def ring_of_eight(block, axis):
    up = [rotate(block, axis, 1)]
    down = [rotate(block, axis, -1)]
    for _ in range(2):
        up.append(rotate(up[-1], axis, 1))
        down.append(rotate(down[-1], axis, -1))
    across = jnp.concatenate([rotate(up[2][:1], axis, 1), rotate(down[2][1:], axis, -1)], axis=0)
    return [block] + up + [across] + down[::-1]


def where_am_i():
    h, x, z = (lax.axis_index(a) for a in REGION)
    yl, c = (lax.axis_index(a) for a in MP)
    return h, x, z, yl, c


def even_count(counts_ref):
    h, x, z, _, _ = where_am_i()
    return counts_ref[h * 32 + x * 8 + (z // 2) * 2]


SMEM = pl.BlockSpec(memory_space=pltpu.SMEM)
VMEM = pl.BlockSpec(memory_space=pltpu.VMEM)
HBM = pl.BlockSpec(memory_space=pltpu.HBM)


def cost(flops, size, special=0):
    return pl.CostEstimate(flops=flops, bytes_accessed=size, transcendentals=special)


def pack_kernel(qkv_ref, out_ref, own_qk, own_vo, sent):
    h = lax.axis_index("h")
    mine = pl.ds(pl.multiple_of(h * HALF, HALF), HALF)
    theirs = pl.ds(pl.multiple_of((1 - h) * HALF, HALF), HALF)
    own_qk[:, :HALF] = qkv_ref[0, :, mine]
    own_qk[:, HALF:] = qkv_ref[1, :, mine]
    own_vo[:, :HALF] = qkv_ref[2, :, mine]
    own_vo[:, HALF : 2 * HALF] = out_ref[:, mine]
    own_vo[:, 2 * HALF :] = out_ref[:, theirs]
    for n in range(3):
        sent[:, n * HALF : (n + 1) * HALF] = qkv_ref[n, :, theirs]
    sent[:, 3 * HALF : 4 * HALF] = out_ref[:, theirs]
    sent[:, 4 * HALF :] = out_ref[:, mine]


def packed(qkv, out):
    return pl.pallas_call(
        pack_kernel,
        in_specs=[VMEM, VMEM],
        out_specs=[VMEM] * 3,
        out_shape=[jax.ShapeDtypeStruct((32, n * HALF), BF) for n in (2, 3, 5)],
        cost_estimate=cost(0, 2**18),
        name="pack",
    )(qkv, out)


def split_kernel(counts_ref, data_ref, sent_ref, kept_ref, sem):
    even = even_count(counts_ref)
    odd = lax.axis_index("z") % 2 == 1
    copies = []
    for s in range(2):
        away = jnp.where(odd, jnp.clip(s - even, 0, 3), 2 + s)
        stays = jnp.where(odd, jnp.clip(2 + s - even, 0, 3), s)
        copies.append(pltpu.make_async_copy(data_ref.at[away], sent_ref.at[s], sem))
        copies.append(pltpu.make_async_copy(data_ref.at[stays], kept_ref.at[s], sem))
    for copy in copies:
        copy.start()
    for copy in copies:
        copy.wait()


def split_tiles(counts, data):
    return pl.pallas_call(
        split_kernel,
        in_specs=[SMEM, HBM],
        out_specs=[VMEM, VMEM],
        out_shape=[jax.ShapeDtypeStruct((2, TOK, NARROW), BF)] * 2,
        scratch_shapes=[pltpu.SemaphoreType.DMA],
        cost_estimate=cost(0, 2**21),
        name="split",
    )(counts, data)


def choose_kernel(counts_ref, kept, came, mod, other_mod, tiles, mods, gate):
    even = even_count(counts_ref)
    odd = lax.axis_index("z") % 2 == 1
    place = lax.axis_index("yl") * 2 + lax.axis_index("c")
    cols = pl.ds(pl.multiple_of(place * NARROW, NARROW), NARROW)
    for s in range(2):
        use_other = jnp.where(odd, 2 + s < even, s >= even)

        @pl.when(use_other)
        def _():
            tiles[s] = came[s]
            mods[s] = other_mod[0]
            gate[s] = other_mod[0, 2:3, cols].astype(F32)

        @pl.when(jnp.logical_not(use_other))
        def _():
            tiles[s] = kept[s]
            mods[s] = mod[0]
            gate[s] = mod[0, 2:3, cols].astype(F32)


def choose(counts, kept, came, mod, other_mod):
    return pl.pallas_call(
        choose_kernel,
        in_specs=[SMEM] + [VMEM] * 4,
        out_specs=[VMEM] * 3,
        out_shape=[
            jax.ShapeDtypeStruct((2, TOK, NARROW), BF),
            jax.ShapeDtypeStruct((2, 3, D), BF),
            jax.ShapeDtypeStruct((2, 1, NARROW), F32),
        ],
        cost_estimate=cost(0, 2**21),
        name="choose",
    )(counts, kept, came, mod, other_mod)


def hidden_kernel(a_ref, b_ref, c_ref, d_ref, mod_ref, out_ref):
    place = lax.axis_index("yl") * 2 + lax.axis_index("c")
    parts = [r[...].astype(F32) for r in (a_ref, b_ref, c_ref, d_ref)]
    mean = sum(jnp.sum(p, axis=-1, keepdims=True) for p in parts) * (1.0 / D)
    parts = [p - mean for p in parts]
    spread = sum(jnp.sum(p * p, axis=-1, keepdims=True) for p in parts) * (1.0 / D)
    scale = lax.rsqrt(spread + 1e-06)
    for j, p in enumerate(parts):
        source = pl.ds(pl.multiple_of((place ^ j) * NARROW, NARROW), NARROW)
        gain = 1.0 + mod_ref[0, 1:2, source].astype(F32)
        value = p * scale * gain + mod_ref[0, 0:1, source].astype(F32)
        out_ref[:, j * NARROW : (j + 1) * NARROW] = value.astype(BF)


def hidden_of(pieces, mods):
    rows = 128
    piece = pl.BlockSpec((rows, NARROW), lambda i: (i, 0))
    return pl.pallas_call(
        hidden_kernel,
        grid=(512 // rows,),
        in_specs=[piece] * 4 + [pl.BlockSpec((1, 3, D), lambda i: (i * rows // TOK, 0, 0))],
        out_specs=pl.BlockSpec((rows, D), lambda i: (i, 0)),
        out_shape=jax.ShapeDtypeStruct((512, D), BF),
        cost_estimate=cost(8 * 512 * D, 4 * 512 * D, 512),
        name="hidden",
    )(*pieces, mods)


def slot_of(hr, xr):
    h, x, _, yl, c = where_am_i()
    px = x ^ xr
    return ((h ^ hr ^ yl) * 2 + ((px // 2) ^ c)) * 2 + px % 2


def attend_kernel(hid_hbm, qk_ref, v0, v1, v2, v3, out_ref, hid_ref, w_ref, hid_sem, sem):
    z = lax.axis_index("z")
    load = pltpu.make_async_copy(hid_hbm, hid_ref, hid_sem)
    load.start()
    copies = []
    for hr in range(2):
        for xr, v in enumerate((v0, v1, v2, v3)):
            slot = slot_of(hr, xr)
            copies.append(
                pltpu.make_async_copy(
                    qk_ref.at[:, xr, hr], w_ref.at[slot, :, :, pl.ds(0, 2 * HALF)], sem
                )
            )
            for s in range(8):
                copies.append(
                    pltpu.make_async_copy(
                        v.at[s, hr],
                        w_ref.at[slot, (z + 8 - s) % 8, :, pl.ds(2 * HALF, HALF)],
                        sem,
                    )
                )
    for copy in copies:
        copy.start()
    load.wait()
    for copy in copies:
        copy.wait()
    weight = w_ref[...].reshape(D, 3 * HALF)
    for t in range(2):
        rows = slice(t * TOK, (t + 1) * TOK)
        proj = jnp.dot(hid_ref[rows, :], weight, preferred_element_type=F32).astype(BF)
        for n in range(2):
            q = proj[:, n * HDIM : (n + 1) * HDIM]
            k = proj[:, HALF + n * HDIM : HALF + (n + 1) * HDIM]
            v = proj[:, 2 * HALF + n * HDIM : 2 * HALF + (n + 1) * HDIM]
            scores = lax.dot_general(
                q, k, (((1,), (1,)), ((), ())), preferred_element_type=F32
            ) * (1.0 / math.sqrt(HDIM))
            top = jnp.max(scores, axis=-1, keepdims=True)
            e = jnp.exp(scores - top)
            probs = (e / jnp.sum(e, axis=-1, keepdims=True)).astype(BF)
            got = jnp.dot(probs, v, preferred_element_type=F32)
            out_ref[rows, n * HDIM : (n + 1) * HDIM] = got.astype(BF)


def attended_of(hidden, qk, vs):
    return pl.pallas_call(
        attend_kernel,
        in_specs=[HBM] * 6,
        out_specs=VMEM,
        out_shape=jax.ShapeDtypeStruct((512, HALF), BF),
        scratch_shapes=[
            pltpu.VMEM((512, D), BF),
            pltpu.VMEM((8, 8, 32, 3 * HALF), BF),
            pltpu.SemaphoreType.DMA,
            pltpu.SemaphoreType.DMA,
        ],
        compiler_params=pltpu.CompilerParams(vmem_limit_bytes=32 * 2**20),
        cost_estimate=cost(
            2 * 512 * D * 768 + 4 * 4 * TOK * TOK * HDIM, 6 * 2**20, 4 * TOK * TOK
        ),
        name="attend",
    )(hidden, qk, *vs)


def project_kernel(far, own_ref, other_ref, o0, o1, o2, o3, *rest):
    keep, send, (w_ref, sem) = rest[:2], rest[2:4], rest[4:]
    h, x, z, yl, c = where_am_i()
    copies = []
    for xr, piece in enumerate((o0, o1, o2, o3)):
        px = x ^ xr
        slot = ((px // 2) ^ c) * 2 + px % 2
        for s in range(8):
            copies.append(
                pltpu.make_async_copy(
                    piece.at[s, yl ^ far ^ h], w_ref.at[slot, (z + 8 - s) % 8], sem
                )
            )
    for copy in copies:
        copy.start()
    for copy in copies:
        copy.wait()
    for b, outs in ((1, send), (0, keep)):
        for f in range(2):
            weight = w_ref[2 * b + f].reshape(HALF, NARROW)
            total = lax.dot_general(
                own_ref[...], weight[:, :HALF], (((1,), (1,)), ((), ())), preferred_element_type=F32
            ) + lax.dot_general(
                other_ref[...], weight[:, HALF:], (((1,), (1,)), ((), ())), preferred_element_type=F32
            )
            outs[f][...] = total.astype(BF)


def partial_of(far, own, other, os):
    got = pl.pallas_call(
        functools.partial(project_kernel, far),
        in_specs=[VMEM, VMEM] + [HBM] * 4,
        out_specs=[VMEM] * 4,
        out_shape=[jax.ShapeDtypeStruct((512, HALF), BF)] * 4,
        scratch_shapes=[pltpu.VMEM((4, 8, 32, NARROW), BF), pltpu.SemaphoreType.DMA],
        compiler_params=pltpu.CompilerParams(vmem_limit_bytes=32 * 2**20),
        cost_estimate=cost(2 * 512 * 512 * 1024, 3 * 2**20),
        name="project",
    )(own, other, *os)
    return got[:2], got[2:]


def place_kernel(counts_ref, own0, own1, other0, other1, out_ref, zero_ref, sem):
    even = even_count(counts_ref)
    parity = lax.axis_index("z") % 2
    zero_ref[...] = jnp.zeros_like(zero_ref)
    waits = []
    for slot in range(4):
        tile = slot + parity * even
        live = jnp.where(parity == 1, tile < 4, slot < even)
        ours = tile // 2 == parity
        for f, (own, other) in enumerate(((own0, other0), (own1, other1))):
            target = out_ref.at[slot, :, pl.ds(f * HALF, HALF)]

            @pl.when(live & ours)
            def _():
                pltpu.make_async_copy(own.at[tile % 2], target, sem).start()

            @pl.when(live & jnp.logical_not(ours))
            def _():
                pltpu.make_async_copy(other.at[tile % 2], target, sem).start()

            @pl.when(jnp.logical_not(live))
            def _():
                pltpu.make_async_copy(zero_ref, target, sem).start()

            waits.append(pltpu.make_async_copy(zero_ref, target, sem))
    for wait in waits:
        wait.wait()


def place_tiles(counts, own, other):
    return pl.pallas_call(
        place_kernel,
        in_specs=[SMEM] + [VMEM] * 4,
        out_specs=HBM,
        out_shape=jax.ShapeDtypeStruct((4, TOK, NARROW), BF),
        scratch_shapes=[pltpu.VMEM((TOK, HALF), BF), pltpu.SemaphoreType.DMA],
        cost_estimate=cost(0, 2**21),
        name="place",
    )(counts, *own, *other)


def mix(earlier, later, share):
    return (1.0 - share) * earlier.astype(F32) + share * later.astype(F32)


def join_columns(grid, region, shares):
    share = shares.reshape(1, W, 1)
    west, east = grid[:, :, :W], grid[:, :, S - W :]
    later = shift(west[0], -1, lambda i: i % 4 != 0)
    earlier = shift(east[1], 1, lambda i: i % 4 != 3)
    place = region % 4
    inner = mix(east[0], west[1], share).astype(BF)
    left = jnp.where(place != 0, mix(earlier, west[0], share).astype(BF), west[0])
    right = jnp.where(place != 3, mix(east[1], later, share).astype(BF), east[1])
    middle = grid[:, :, W : S - W]
    first = jnp.concatenate([left, middle[0], inner], axis=1)
    second = jnp.concatenate([inner, middle[1], right], axis=1)
    return jnp.stack([first, second])


def join_rows(grid, region, shares):
    share = shares.reshape(1, W, 1, 1)
    north, south = grid[:, :W], grid[:, S - W :]
    later = shift(north, -4, lambda i: True)
    earlier = shift(south, 4, lambda i: True)
    top = jnp.where(region >= 4, mix(earlier, north, share).astype(BF), north)
    bottom = jnp.where(region < 60, mix(south, later, share).astype(BF), south)
    return jnp.concatenate([top, grid[:, W : S - W], bottom], axis=1)


def on_device(tile_data, tile_counts, modulation, qkv_weight, out_weight, blend_weights):
    h, x, z, _, _ = where_am_i()
    region = h * 32 + x * 8 + z

    own_qk, own_vo, sent = packed(qkv_weight.transpose(1, 0, 2), out_weight)
    came = xor_swap(sent, "h", 1)
    qk_block = jnp.stack([own_qk, came[:, : 2 * HALF]])
    vo_block = jnp.stack([own_vo, came[:, 2 * HALF :]])
    qk_all = lax.all_gather(jnp.stack(ring_of_four(qk_block, "x", 0)), "z", axis=0)
    vo_z = ring_of_eight(vo_block, "z")
    v_all = ring_of_four(jnp.stack([b[..., :HALF] for b in vo_z]), "x", 0)
    o_all = ring_of_four(jnp.stack([b[..., HALF:] for b in vo_z]), "x", 0)

    away, kept = split_tiles(tile_counts, tile_data)
    tiles, mods, gate = choose(
        tile_counts, kept, xor_swap(away, "z", 1), modulation, xor_swap(modulation, "z", 1)
    )

    ring = ("h", "yl")
    mine = tiles.reshape(512, NARROW)
    _, near, across, side = ring_of_four(mine, ring, 0)
    mods_across = xor_swap(mods, "h", 1)
    hid_other = hidden_of(
        (across, xor_swap(across, "c", 1), side, xor_swap(side, "c", 1)), mods_across
    )
    hid_own = hidden_of((mine, xor_swap(mine, "c", 1), near, xor_swap(near, "c", 1)), mods)

    att_sent = attended_of(hid_other, qk_all, v_all)
    att_other = opposite(xor_swap(att_sent, ring, 1), xor_swap(att_sent, ring, 3), ring, 0)
    att_own = attended_of(hid_own, qk_all, v_all)

    far_keep, far_send = partial_of(1, att_own, att_other, o_all)
    far = [
        xor_swap((k.astype(F32) + xor_swap(s, "c", 1).astype(F32)).astype(BF), "yl", 1)
        for k, s in zip(far_keep, far_send)
    ]
    keep, send = partial_of(0, att_own, att_other, o_all)
    own, other = [], []
    for f in range(2):
        cols = slice(f * HALF, (f + 1) * HALF)
        summed = sum(p.astype(F32) for p in (keep[f], xor_swap(send[f], "c", 1), far[f]))
        updated = tiles[:, :, cols].astype(F32) + gate[:, :, cols] * summed.reshape(2, TOK, HALF)
        grid = updated.astype(BF).reshape(2, S, S, HALF)
        grid = join_columns(grid, region, blend_weights)
        grid = join_rows(grid, region, blend_weights).reshape(2, TOK, HALF)
        own.append(grid)
        other.append(xor_swap(grid, "z", 1))
    return place_tiles(tile_counts, own, other)


def solution(mesh):
    fine = Mesh(mesh.devices.reshape(2, 4, 8, 2, 2), REGION + MP)
    return jax.shard_map(
        on_device,
        mesh=fine,
        in_specs=(
            P(REGION, None, MP),
            P(),
            P(REGION, None, None),
            P(REGION, None, MP),
            P(REGION, MP),
            P(),
        ),
        out_specs=P(REGION, None, MP),
        check_vma=False,
    )
```

```python
import functools
import math

import jax
import jax.numpy as jnp
from jax import lax
from jax.experimental import pallas as pl
from jax.experimental.pallas import tpu as pltpu
from jax.sharding import Mesh, PartitionSpec as P

D = 2048
HDIM = 128
S = 16
W = 6
TOK = 256
NARROW = 512
HALF = 256
REGION = ("h", "x", "z")
MP = ("yl", "c")
BF = jnp.bfloat16
F32 = jnp.float32


def xor_swap(block, axis, bit):
    size = math.prod(lax.axis_size(a) for a in ((axis,) if isinstance(axis, str) else axis))
    return lax.ppermute(block, axis, [(i, i ^ bit) for i in range(size)])


def rotate(block, axis, step):
    size = lax.axis_size(axis)
    return lax.ppermute(block, axis, [(i, (i + step) % size) for i in range(size)])


def shift(block, distance, allowed):
    route = [(i, i + distance) for i in range(64) if 0 <= i + distance < 64 and allowed(i)]
    return lax.ppermute(block, REGION, route)


def opposite(near, side, axis, split_axis):
    size = near.shape[split_axis]
    first = xor_swap(lax.slice_in_dim(side, 0, size // 2, axis=split_axis), axis, 1)
    second = xor_swap(lax.slice_in_dim(near, size // 2, size, axis=split_axis), axis, 3)
    return jnp.concatenate([first, second], axis=split_axis)


def ring_of_four(block, axis, split_axis):
    near = xor_swap(block, axis, 1)
    side = xor_swap(block, axis, 3)
    return block, near, opposite(near, side, axis, split_axis), side


def where_am_i():
    h, x, z = (lax.axis_index(a) for a in REGION)
    yl, c = (lax.axis_index(a) for a in MP)
    return h, x, z, yl, c


def even_count(counts_ref):
    h, x, z, _, _ = where_am_i()
    return counts_ref[h * 32 + x * 8 + (z // 2) * 2]


SMEM = pl.BlockSpec(memory_space=pltpu.SMEM)
VMEM = pl.BlockSpec(memory_space=pltpu.VMEM)
HBM = pl.BlockSpec(memory_space=pltpu.HBM)


def cost(flops, size, special=0):
    return pl.CostEstimate(flops=flops, bytes_accessed=size, transcendentals=special)


def pack_kernel(qkv_ref, out_ref, own, sent):
    h = lax.axis_index("h")
    mine = pl.ds(pl.multiple_of(h * HALF, HALF), HALF)
    theirs = pl.ds(pl.multiple_of((1 - h) * HALF, HALF), HALF)
    for n in range(3):
        own[n] = qkv_ref[n, :, mine]
        sent[n] = qkv_ref[n, :, theirs]
    own[3] = out_ref[:, mine]
    own[4] = out_ref[:, theirs]
    sent[3] = out_ref[:, theirs]
    sent[4] = out_ref[:, mine]


def packed(qkv, out):
    return pl.pallas_call(
        pack_kernel,
        in_specs=[VMEM, VMEM],
        out_specs=[VMEM] * 2,
        out_shape=[jax.ShapeDtypeStruct((5, 32, HALF), BF)] * 2,
        cost_estimate=cost(0, 2**18),
        name="pack",
    )(qkv, out)


def split_kernel(counts_ref, data_ref, sent_ref, kept_ref, sem):
    even = even_count(counts_ref)
    odd = lax.axis_index("z") % 2 == 1
    copies = []
    for s in range(2):
        away = jnp.where(odd, jnp.clip(s - even, 0, 3), 2 + s)
        stays = jnp.where(odd, jnp.clip(2 + s - even, 0, 3), s)
        copies.append(pltpu.make_async_copy(data_ref.at[away], sent_ref.at[s], sem))
        copies.append(pltpu.make_async_copy(data_ref.at[stays], kept_ref.at[s], sem))
    for copy in copies:
        copy.start()
    for copy in copies:
        copy.wait()


def split_tiles(counts, data):
    return pl.pallas_call(
        split_kernel,
        in_specs=[SMEM, HBM],
        out_specs=[VMEM, VMEM],
        out_shape=[jax.ShapeDtypeStruct((2, TOK, NARROW), BF)] * 2,
        scratch_shapes=[pltpu.SemaphoreType.DMA],
        cost_estimate=cost(0, 2**21),
        name="split",
    )(counts, data)


def choose_kernel(counts_ref, kept, came, mod, other_mod, tiles, mods, gate):
    even = even_count(counts_ref)
    odd = lax.axis_index("z") % 2 == 1
    place = lax.axis_index("yl") * 2 + lax.axis_index("c")
    cols = pl.ds(pl.multiple_of(place * NARROW, NARROW), NARROW)
    for s in range(2):
        use_other = jnp.where(odd, 2 + s < even, s >= even)

        @pl.when(use_other)
        def _():
            tiles[s] = came[s]
            mods[s] = other_mod[0]
            gate[s] = other_mod[0, 2:3, cols].astype(F32)

        @pl.when(jnp.logical_not(use_other))
        def _():
            tiles[s] = kept[s]
            mods[s] = mod[0]
            gate[s] = mod[0, 2:3, cols].astype(F32)


def choose(counts, kept, came, mod, other_mod):
    return pl.pallas_call(
        choose_kernel,
        in_specs=[SMEM] + [VMEM] * 4,
        out_specs=[VMEM] * 3,
        out_shape=[
            jax.ShapeDtypeStruct((2, TOK, NARROW), BF),
            jax.ShapeDtypeStruct((2, 3, D), BF),
            jax.ShapeDtypeStruct((2, 1, NARROW), F32),
        ],
        cost_estimate=cost(0, 2**21),
        name="choose",
    )(counts, kept, came, mod, other_mod)


def slot_of(hr, xr):
    h, x, _, yl, c = where_am_i()
    px = x ^ xr
    return ((h ^ hr ^ yl) * 2 + ((px // 2) ^ c)) * 2 + px % 2


def normalise_rows(rows, part_ref, mod_ref, hid_ref):
    place = lax.axis_index("yl") * 2 + lax.axis_index("c")
    parts = [part_ref[j, rows, :].astype(F32) for j in range(4)]
    mean = sum(jnp.sum(p, axis=-1, keepdims=True) for p in parts) * (1.0 / D)
    parts = [p - mean for p in parts]
    spread = sum(jnp.sum(p * p, axis=-1, keepdims=True) for p in parts) * (1.0 / D)
    scale = lax.rsqrt(spread + 1e-06)
    tile = rows.start // TOK
    for j, p in enumerate(parts):
        source = pl.ds(pl.multiple_of((place ^ j) * NARROW, NARROW), NARROW)
        gain = 1.0 + mod_ref[tile, 1:2, source].astype(F32)
        value = p * scale * gain + mod_ref[tile, 0:1, source].astype(F32)
        hid_ref[rows, j * NARROW : (j + 1) * NARROW] = value.astype(BF)


def attend_kernel(
    a_hbm, b_hbm, c_hbm, d_hbm, mod_ref, g_ref, out_ref, part_ref, hid_ref, w_ref, part_sem, sem
):
    loads = [
        pltpu.make_async_copy(piece, part_ref.at[j], part_sem)
        for j, piece in enumerate((a_hbm, b_hbm, c_hbm, d_hbm))
    ]
    copies = []
    for hr in range(2):
        for xr in range(4):
            slot = slot_of(hr, xr)
            for n in range(3):
                copies.append(
                    pltpu.make_async_copy(
                        g_ref.at[:, (xr * 2 + hr) * 3 + n],
                        w_ref.at[slot, :, :, pl.ds(n * HALF, HALF)],
                        sem,
                    )
                )
    for copy in loads + copies:
        copy.start()
    for load in loads:
        load.wait()
    for r in range(0, 2 * TOK, 64):
        normalise_rows(slice(r, r + 64), part_ref, mod_ref, hid_ref)
    for copy in copies:
        copy.wait()
    weight = w_ref[...].reshape(D, 3 * HALF)
    for t in range(2):
        rows = slice(t * TOK, (t + 1) * TOK)
        proj = jnp.dot(hid_ref[rows, :], weight, preferred_element_type=F32).astype(BF)
        for n in range(2):
            q = proj[:, n * HDIM : (n + 1) * HDIM]
            k = proj[:, HALF + n * HDIM : HALF + (n + 1) * HDIM]
            v = proj[:, 2 * HALF + n * HDIM : 2 * HALF + (n + 1) * HDIM]
            scores = lax.dot_general(
                q, k, (((1,), (1,)), ((), ())), preferred_element_type=F32
            ) * (1.0 / math.sqrt(HDIM))
            top = jnp.max(scores, axis=-1, keepdims=True)
            e = jnp.exp(scores - top)
            probs = (e / jnp.sum(e, axis=-1, keepdims=True)).astype(BF)
            got = jnp.dot(probs, v, preferred_element_type=F32)
            out_ref[rows, n * HDIM : (n + 1) * HDIM] = got.astype(BF)


def attended_of(pieces, mods, gathered):
    return pl.pallas_call(
        attend_kernel,
        in_specs=[HBM] * 4 + [VMEM, HBM],
        out_specs=VMEM,
        out_shape=jax.ShapeDtypeStruct((512, HALF), BF),
        scratch_shapes=[
            pltpu.VMEM((4, 512, NARROW), BF),
            pltpu.VMEM((512, D), BF),
            pltpu.VMEM((8, 8, 32, 3 * HALF), BF),
            pltpu.SemaphoreType.DMA,
            pltpu.SemaphoreType.DMA,
        ],
        compiler_params=pltpu.CompilerParams(vmem_limit_bytes=60 * 2**20),
        cost_estimate=cost(
            2 * 512 * D * 768 + 4 * 4 * TOK * TOK * HDIM, 6 * 2**20, 4 * TOK * TOK
        ),
        name="attend",
    )(*pieces, mods, gathered)


def project_kernel(far, own_ref, other_ref, o0, o1, o2, o3, keep_ref, send_ref, w_ref, sem):
    h, x, _, yl, c = where_am_i()
    copies = []
    for xr, piece in enumerate((o0, o1, o2, o3)):
        px = x ^ xr
        slot = ((px // 2) ^ c) * 2 + px % 2
        for n in range(2):
            copies.append(
                pltpu.make_async_copy(
                    piece.at[:, (yl ^ far ^ h) * 2 + n],
                    w_ref.at[slot, :, :, pl.ds(n * HALF, HALF)],
                    sem,
                )
            )
    for copy in copies:
        copy.start()
    for copy in copies:
        copy.wait()
    for b, out_ref in ((1, send_ref), (0, keep_ref)):
        weight = w_ref[2 * b : 2 * b + 2].reshape(NARROW, NARROW)
        total = lax.dot_general(
            own_ref[...], weight[:, :HALF], (((1,), (1,)), ((), ())), preferred_element_type=F32
        ) + lax.dot_general(
            other_ref[...], weight[:, HALF:], (((1,), (1,)), ((), ())), preferred_element_type=F32
        )
        out_ref[...] = total.astype(BF)


def partial_of(far, own, other, os):
    return pl.pallas_call(
        functools.partial(project_kernel, far),
        in_specs=[VMEM, VMEM] + [HBM] * 4,
        out_specs=[VMEM] * 2,
        out_shape=[jax.ShapeDtypeStruct((512, NARROW), BF)] * 2,
        scratch_shapes=[pltpu.VMEM((4, 8, 32, NARROW), BF), pltpu.SemaphoreType.DMA],
        compiler_params=pltpu.CompilerParams(vmem_limit_bytes=16 * 2**20),
        cost_estimate=cost(2 * 512 * 512 * 1024, 3 * 2**20),
        name="project",
    )(own, other, *os)


def place_kernel(counts_ref, own, other, out_ref, zero_ref, sem):
    even = even_count(counts_ref)
    parity = lax.axis_index("z") % 2
    zero_ref[...] = jnp.zeros_like(zero_ref)
    waits = []
    for slot in range(4):
        tile = slot + parity * even
        live = jnp.where(parity == 1, tile < 4, slot < even)
        ours = tile // 2 == parity
        target = out_ref.at[slot]

        @pl.when(live & ours)
        def _():
            pltpu.make_async_copy(own.at[tile % 2], target, sem).start()

        @pl.when(live & jnp.logical_not(ours))
        def _():
            pltpu.make_async_copy(other.at[tile % 2], target, sem).start()

        @pl.when(jnp.logical_not(live))
        def _():
            pltpu.make_async_copy(zero_ref, target, sem).start()

        waits.append(pltpu.make_async_copy(zero_ref, target, sem))
    for wait in waits:
        wait.wait()


def place_tiles(counts, own, other):
    return pl.pallas_call(
        place_kernel,
        in_specs=[SMEM, VMEM, VMEM],
        out_specs=HBM,
        out_shape=jax.ShapeDtypeStruct((4, TOK, NARROW), BF),
        scratch_shapes=[pltpu.VMEM((TOK, NARROW), BF), pltpu.SemaphoreType.DMA],
        cost_estimate=cost(0, 2**21),
        name="place",
    )(counts, own, other)


def mix(earlier, later, share):
    return ((1.0 - share) * earlier.astype(F32) + share * later.astype(F32)).astype(BF)


def join_rows(strip, region, shares):
    count = strip.shape[1]
    share = shares.reshape(W, 1, 1)
    top, bottom = strip[:W], strip[S - W :]
    later = shift(top.reshape(W * count, NARROW), -4, lambda i: True)
    earlier = shift(bottom.reshape(W * count, NARROW), 4, lambda i: True)
    later, earlier = lax.optimization_barrier((later, earlier))
    top = jnp.where(region >= 4, mix(earlier.reshape(W, count, NARROW), top, share), top)
    bottom = jnp.where(region < 60, mix(bottom, later.reshape(W, count, NARROW), share), bottom)
    return jnp.concatenate([top, strip[W : S - W], bottom], axis=0)


def blend(tiles, region, shares):
    first, second = tiles[0], tiles[1]
    share = shares.reshape(1, W, 1)
    west, east = first[:, :W], second[:, S - W :]
    later = shift(west, -1, lambda i: i % 4 != 0)
    earlier = shift(east, 1, lambda i: i % 4 != 3)
    later, earlier = lax.optimization_barrier((later, earlier))
    place = region % 4
    left = jnp.where(place != 0, mix(earlier, west, share), west)
    right = jnp.where(place != 3, mix(east, later, share), east)
    inner = mix(first[:, S - W :], second[:, :W], share)
    strip = jnp.concatenate(
        [left, first[:, W : S - W], inner, second[:, W : S - W], right], axis=1
    )
    strip = join_rows(strip, region, shares)
    return jnp.stack([strip[:, :S], strip[:, S - W :]])


def on_device(tile_data, tile_counts, modulation, qkv_weight, out_weight, blend_weights):
    h, x, z, _, _ = where_am_i()
    region = h * 32 + x * 8 + z

    own_blocks, sent_blocks = packed(qkv_weight.transpose(1, 0, 2), out_weight)
    came_blocks = xor_swap(sent_blocks, "h", 1)

    tile_data, sent_blocks = lax.optimization_barrier((tile_data, sent_blocks))
    away, kept = split_tiles(tile_counts, tile_data)
    came = xor_swap(away, "z", 1)
    came_mod = xor_swap(modulation, "z", 1)

    came_blocks, kept = lax.optimization_barrier((came_blocks, kept))
    qkv = jnp.concatenate([own_blocks[:3], came_blocks[:3]])
    pieces = [qkv] + [xor_swap(qkv, "x", bit) for bit in (1, 2, 3)]
    block = jnp.concatenate(pieces + [own_blocks[3:], came_blocks[3:]])
    gathered = lax.all_gather(block, "z", axis=0)

    tiles, mods, gate = choose(tile_counts, kept, came, modulation, came_mod)
    ring = ("h", "yl")
    mine = tiles.reshape(512, NARROW)
    _, near, across, side = ring_of_four(mine, ring, 0)
    mods_across = xor_swap(mods, "h", 1)
    own_pieces = (mine, xor_swap(mine, "c", 1), near, xor_swap(near, "c", 1))
    other_pieces = (across, xor_swap(across, "c", 1), side, xor_swap(side, "c", 1))

    o_block = gathered[:, 24:]
    o_near, o_side = xor_swap(o_block, "x", 1), xor_swap(o_block, "x", 3)
    att_sent = attended_of(other_pieces, mods_across, gathered)
    att_near, att_side = xor_swap(att_sent, ring, 1), xor_swap(att_sent, ring, 3)
    att_own = attended_of(own_pieces, mods, gathered)
    o_near, o_side, att_near, att_side, att_own = lax.optimization_barrier(
        (o_near, o_side, att_near, att_side, att_own)
    )
    att_other = opposite(att_near, att_side, ring, 0)
    o_all = (o_block, o_near, opposite(o_near, o_side, "x", 0), o_side)

    far_keep, far_send = partial_of(1, att_own, att_other, o_all)
    far = (far_keep.astype(F32) + xor_swap(far_send, "c", 1).astype(F32)).astype(BF)
    far = xor_swap(far, "yl", 1)
    keep, send = partial_of(0, att_own, att_other, o_all)
    summed = keep.astype(F32) + xor_swap(send, "c", 1).astype(F32) + far.astype(F32)
    updated = tiles.astype(F32) + gate * summed.reshape(2, TOK, NARROW)
    updated = updated.astype(BF).reshape(2, S, S, NARROW)
    finished = blend(updated, region, blend_weights).reshape(2, TOK, NARROW)
    return place_tiles(tile_counts, finished, xor_swap(finished, "z", 1))


def solution(mesh):
    fine = Mesh(mesh.devices.reshape(2, 4, 8, 2, 2), REGION + MP)
    return jax.shard_map(
        on_device,
        mesh=fine,
        in_specs=(
            P(REGION, None, MP),
            P(),
            P(REGION, None, None),
            P(REGION, None, MP),
            P(REGION, MP),
            P(),
        ),
        out_specs=P(REGION, None, MP),
        check_vma=False,
    )
```

```python
import functools
import math

import jax
import jax.numpy as jnp
from jax import lax
from jax.experimental import pallas as pl
from jax.experimental.pallas import tpu as pltpu
from jax.sharding import Mesh, PartitionSpec as P

D = 2048
HDIM = 128
S = 16
W = 6
TOK = 256
NARROW = 512
HALF = 256
REGION = ("h", "x", "z")
MP = ("yl", "c")
BF = jnp.bfloat16
F32 = jnp.float32


def xor_swap(block, axis, bit):
    size = math.prod(lax.axis_size(a) for a in ((axis,) if isinstance(axis, str) else axis))
    return lax.ppermute(block, axis, [(i, i ^ bit) for i in range(size)])


def rotate(block, axis, step):
    size = lax.axis_size(axis)
    return lax.ppermute(block, axis, [(i, (i + step) % size) for i in range(size)])


def trade(block, distance, lower):
    route = []
    for i in range(64):
        j = i + distance if lower(i) else i - distance
        if 0 <= j < 64:
            route.append((i, j))
    return lax.ppermute(block, REGION, route)


def opposite(near, side, axis, split_axis):
    size = near.shape[split_axis]
    first = xor_swap(lax.slice_in_dim(side, 0, size // 2, axis=split_axis), axis, 1)
    second = xor_swap(lax.slice_in_dim(near, size // 2, size, axis=split_axis), axis, 3)
    return jnp.concatenate([first, second], axis=split_axis)


def ring_of_four(block, axis, split_axis):
    near = xor_swap(block, axis, 1)
    side = xor_swap(block, axis, 3)
    return block, near, opposite(near, side, axis, split_axis), side


def where_am_i():
    h, x, z = (lax.axis_index(a) for a in REGION)
    yl, c = (lax.axis_index(a) for a in MP)
    return h, x, z, yl, c


def even_count(counts_ref):
    h, x, z, _, _ = where_am_i()
    return counts_ref[h * 32 + x * 8 + (z // 2) * 2]


SMEM = pl.BlockSpec(memory_space=pltpu.SMEM)
VMEM = pl.BlockSpec(memory_space=pltpu.VMEM)
HBM = pl.BlockSpec(memory_space=pltpu.HBM)


def cost(flops, size, special=0):
    return pl.CostEstimate(flops=flops, bytes_accessed=size, transcendentals=special)


def pack_kernel(qkv_ref, out_ref, own, sent):
    h = lax.axis_index("h")
    mine = pl.ds(pl.multiple_of(h * HALF, HALF), HALF)
    theirs = pl.ds(pl.multiple_of((1 - h) * HALF, HALF), HALF)
    for n in range(3):
        own[n] = qkv_ref[n, :, mine]
        sent[n] = qkv_ref[n, :, theirs]
    for n in range(2):
        own[3 + n] = out_ref[:, n * HALF : (n + 1) * HALF]
        sent[3 + n] = out_ref[:, n * HALF : (n + 1) * HALF]


def packed(qkv, out):
    return pl.pallas_call(
        pack_kernel,
        in_specs=[VMEM] * 2,
        out_specs=[VMEM] * 2,
        out_shape=[jax.ShapeDtypeStruct((5, 32, HALF), BF)] * 2,
        cost_estimate=cost(0, 2**18),
        compiler_params=pltpu.CompilerParams(vmem_limit_bytes=8 * 2**20),
        name="pack",
    )(qkv, out)


def split_kernel(counts_ref, data_ref, sent_ref, kept_ref, sem):
    even = even_count(counts_ref)
    odd = lax.axis_index("z") % 2 == 1
    copies = []
    for s in range(2):
        away = jnp.where(odd, jnp.clip(s - even, 0, 3), 2 + s)
        stays = jnp.where(odd, jnp.clip(2 + s - even, 0, 3), s)
        copies.append(pltpu.make_async_copy(data_ref.at[away], sent_ref.at[s], sem))
        copies.append(pltpu.make_async_copy(data_ref.at[stays], kept_ref.at[s], sem))
    for copy in copies:
        copy.start()
    for copy in copies:
        copy.wait()


def split_tiles(counts, data):
    return pl.pallas_call(
        split_kernel,
        in_specs=[SMEM, HBM],
        out_specs=[VMEM, VMEM],
        out_shape=[jax.ShapeDtypeStruct((2, TOK, NARROW), BF)] * 2,
        scratch_shapes=[pltpu.SemaphoreType.DMA],
        cost_estimate=cost(0, 2**21),
        compiler_params=pltpu.CompilerParams(vmem_limit_bytes=12 * 2**20),
        name="split",
    )(counts, data)


def choose_kernel(counts_ref, kept, came, mod, other_mod, tiles, mods, gate):
    even = even_count(counts_ref)
    odd = lax.axis_index("z") % 2 == 1
    place = lax.axis_index("yl") * 2 + lax.axis_index("c")
    cols = pl.ds(pl.multiple_of(place * NARROW, NARROW), NARROW)
    for s in range(2):
        use_other = jnp.where(odd, 2 + s < even, s >= even)

        @pl.when(use_other)
        def _():
            tiles[s] = came[s]
            mods[s] = other_mod[0]
            gate[s] = other_mod[0, 2:3, cols].astype(F32)

        @pl.when(jnp.logical_not(use_other))
        def _():
            tiles[s] = kept[s]
            mods[s] = mod[0]
            gate[s] = mod[0, 2:3, cols].astype(F32)


def choose(counts, kept, came, mod, other_mod):
    return pl.pallas_call(
        choose_kernel,
        in_specs=[SMEM] + [VMEM] * 4,
        out_specs=[VMEM] * 3,
        out_shape=[
            jax.ShapeDtypeStruct((2, TOK, NARROW), BF),
            jax.ShapeDtypeStruct((2, 3, D), BF),
            jax.ShapeDtypeStruct((2, 1, NARROW), F32),
        ],
        cost_estimate=cost(0, 2**21),
        compiler_params=pltpu.CompilerParams(vmem_limit_bytes=12 * 2**20),
        name="choose",
    )(counts, kept, came, mod, other_mod)


def hidden_kernel(a_ref, b_ref, c_ref, d_ref, mod_ref, out_ref):
    place = lax.axis_index("yl") * 2 + lax.axis_index("c")
    parts = [r[...].astype(F32) for r in (a_ref, b_ref, c_ref, d_ref)]
    mean = sum(jnp.sum(p, axis=-1, keepdims=True) for p in parts) * (1.0 / D)
    parts = [p - mean for p in parts]
    spread = sum(jnp.sum(p * p, axis=-1, keepdims=True) for p in parts) * (1.0 / D)
    scale = lax.rsqrt(spread + 1e-06)
    for j, p in enumerate(parts):
        source = pl.ds(pl.multiple_of((place ^ j) * NARROW, NARROW), NARROW)
        gain = 1.0 + mod_ref[0, 1:2, source].astype(F32)
        value = p * scale * gain + mod_ref[0, 0:1, source].astype(F32)
        out_ref[:, j * NARROW : (j + 1) * NARROW] = value.astype(BF)


def hidden_of(pieces, mods):
    rows = 256
    piece = pl.BlockSpec((rows, NARROW), lambda i: (i, 0))
    return pl.pallas_call(
        hidden_kernel,
        grid=(512 // rows,),
        in_specs=[piece] * 4 + [pl.BlockSpec((1, 3, D), lambda i: (i * rows // TOK, 0, 0))],
        out_specs=pl.BlockSpec((rows, D), lambda i: (i, 0)),
        out_shape=jax.ShapeDtypeStruct((512, D), BF),
        cost_estimate=cost(8 * 512 * D, 4 * 512 * D, 512),
        compiler_params=pltpu.CompilerParams(vmem_limit_bytes=24 * 2**20),
        name="hidden",
    )(*pieces, mods)


def attend_kernel(hid_hbm, g_ref, out_ref, hid_ref, w_ref, total_ref, sem):
    h, x, _, yl, c = where_am_i()
    copies = []
    for j in range(4):
        cols = pl.ds(j * NARROW, NARROW)
        group = [pltpu.make_async_copy(hid_hbm.at[:, cols], hid_ref.at[:, cols], sem.at[j])]
        hr = (yl ^ (j // 2)) ^ h
        for half in range(2):
            xr = ((c ^ (j % 2)) * 2 + half) ^ x
            for n in range(3):
                group.append(
                    pltpu.make_async_copy(
                        g_ref.at[:, (xr * 2 + hr) * 3 + n],
                        w_ref.at[j, half, :, :, pl.ds(n * HALF, HALF)],
                        sem.at[j],
                    )
                )
        for copy in group:
            copy.start()
        copies.append(group)
    for j, group in enumerate(copies):
        for copy in group:
            copy.wait()
        part = jnp.dot(
            hid_ref[:, j * NARROW : (j + 1) * NARROW],
            w_ref[j].reshape(NARROW, 3 * HALF),
            preferred_element_type=F32,
        )
        if j == 0:
            total_ref[...] = part
        elif j < 3:
            total_ref[...] += part
    proj = (total_ref[...] + part).astype(BF)

    def block(t, kind, n):
        start = kind * HALF + n * HDIM
        return proj[t * TOK : (t + 1) * TOK, start : start + HDIM]

    units = [(t, n) for t in range(2) for n in range(2)]
    scores = [
        lax.dot_general(
            block(t, 0, n), block(t, 1, n), (((1,), (1,)), ((), ())), preferred_element_type=F32
        )
        * (1.0 / math.sqrt(HDIM))
        for t, n in units
    ]
    exps = [jnp.exp(s - jnp.max(s, axis=-1, keepdims=True)) for s in scores]
    for e, (t, n) in zip(exps, units):
        got = jnp.dot(e.astype(BF), block(t, 2, n), preferred_element_type=F32)
        got = got / jnp.sum(e, axis=-1, keepdims=True)
        out_ref[t * TOK : (t + 1) * TOK, n * HDIM : (n + 1) * HDIM] = got.astype(BF)


def attended_of(hidden, gathered):
    return pl.pallas_call(
        attend_kernel,
        in_specs=[HBM] * 2,
        out_specs=VMEM,
        out_shape=jax.ShapeDtypeStruct((512, HALF), BF),
        scratch_shapes=[
            pltpu.VMEM((512, D), BF),
            pltpu.VMEM((4, 2, 8, 32, 3 * HALF), BF),
            pltpu.VMEM((512, 3 * HALF), F32),
            pltpu.SemaphoreType.DMA((4,)),
        ],
        compiler_params=pltpu.CompilerParams(vmem_limit_bytes=60 * 2**20),
        cost_estimate=cost(
            2 * (2 * 512 * D * 768 + 4 * 4 * TOK * TOK * HDIM), 6 * 2**20, 4 * TOK * TOK
        ),
        name="attend",
    )(hidden, gathered)


def project_kernel(a_ref, b_ref, c_ref, d_ref, o0, o1, o2, o3, keep_ref, send_ref, w_ref, sem):
    h, x, _, _, c = where_am_i()
    copies = []
    for xr, piece in enumerate((o0, o1, o2, o3)):
        px = x ^ xr
        slot = ((px // 2) ^ c) * 2 + px % 2
        for j in range(4):
            block = (j % 2) * 2 + (h ^ (j // 2))
            copies.append(
                pltpu.make_async_copy(
                    piece.at[:, block], w_ref.at[slot, :, :, pl.ds(j * HALF, HALF)], sem
                )
            )
    for copy in copies:
        copy.start()
    for copy in copies:
        copy.wait()
    attended = jnp.concatenate([r[...] for r in (a_ref, b_ref, c_ref, d_ref)], axis=1)
    for b, out_ref in ((1, send_ref), (0, keep_ref)):
        weight = w_ref[2 * b : 2 * b + 2].reshape(NARROW, 4 * HALF)
        total = lax.dot_general(
            attended, weight, (((1,), (1,)), ((), ())), preferred_element_type=F32
        )
        out_ref[...] = total.astype(out_ref.dtype)


def partial_of(attended, os):
    return pl.pallas_call(
        project_kernel,
        in_specs=[VMEM] * 4 + [HBM] * 4,
        out_specs=[VMEM] * 2,
        out_shape=[
            jax.ShapeDtypeStruct((512, NARROW), F32),
            jax.ShapeDtypeStruct((512, NARROW), BF),
        ],
        scratch_shapes=[pltpu.VMEM((4, 8, 32, 4 * HALF), BF), pltpu.SemaphoreType.DMA],
        compiler_params=pltpu.CompilerParams(vmem_limit_bytes=16 * 2**20),
        cost_estimate=cost(2 * 512 * 1024 * 1024, 4 * 2**20),
        name="project",
    )(*attended, *os)


def place_kernel(counts_ref, own, other, out_ref, zero_ref, sem):
    even = even_count(counts_ref)
    parity = lax.axis_index("z") % 2
    zero_ref[...] = jnp.zeros_like(zero_ref)
    waits = []
    for slot in range(4):
        tile = slot + parity * even
        live = jnp.where(parity == 1, tile < 4, slot < even)
        ours = tile // 2 == parity
        target = out_ref.at[slot]

        @pl.when(live & ours)
        def _():
            pltpu.make_async_copy(own.at[tile % 2], target, sem).start()

        @pl.when(live & jnp.logical_not(ours))
        def _():
            pltpu.make_async_copy(other.at[tile % 2], target, sem).start()

        @pl.when(jnp.logical_not(live))
        def _():
            pltpu.make_async_copy(zero_ref, target, sem).start()

        waits.append(pltpu.make_async_copy(zero_ref, target, sem))
    for wait in waits:
        wait.wait()


def place_tiles(counts, own, other):
    return pl.pallas_call(
        place_kernel,
        in_specs=[SMEM, VMEM, VMEM],
        out_specs=HBM,
        out_shape=jax.ShapeDtypeStruct((4, TOK, NARROW), BF),
        scratch_shapes=[pltpu.VMEM((TOK, NARROW), BF), pltpu.SemaphoreType.DMA],
        cost_estimate=cost(0, 2**21),
        compiler_params=pltpu.CompilerParams(vmem_limit_bytes=12 * 2**20),
        name="place",
    )(counts, own, other)


def mix(earlier, later, share):
    return ((1.0 - share) * earlier.astype(F32) + share * later.astype(F32)).astype(BF)


def join_rows(strip, region, shares):
    count = strip.shape[1]
    share = shares.reshape(W, 1, 1)
    top, bottom = strip[:W], strip[S - W :]
    north, south = top.reshape(W * count, NARROW), bottom.reshape(W * count, NARROW)
    first = region % 8 < 4
    same = trade(jnp.where(first, south, north), 4, lambda i: i % 8 < 4)
    cross = trade(jnp.where(first, north, south), 4, lambda i: i % 8 >= 4)
    same, cross = lax.optimization_barrier((same, cross))
    later, earlier = jnp.where(first, same, cross), jnp.where(first, cross, same)
    top = jnp.where(region >= 4, mix(earlier.reshape(W, count, NARROW), top, share), top)
    bottom = jnp.where(region < 60, mix(bottom, later.reshape(W, count, NARROW), share), bottom)
    return jnp.concatenate([top, strip[W : S - W], bottom], axis=0)


def blend(tiles, region, shares):
    first, second = tiles[0], tiles[1]
    share = shares.reshape(1, W, 1)
    west, east = first[:, :W], second[:, S - W :]
    odd = region % 2 == 1
    near = trade(jnp.where(odd, west, east), 1, lambda i: i % 2 == 0)
    across = trade(jnp.where(odd, east, west), 1, lambda i: i % 2 == 1)
    near, across = lax.optimization_barrier((near, across))
    later, earlier = jnp.where(odd, across, near), jnp.where(odd, near, across)
    place = region % 4
    left = jnp.where(place != 0, mix(earlier, west, share), west)
    right = jnp.where(place != 3, mix(east, later, share), east)
    inner = mix(first[:, S - W :], second[:, :W], share)
    strip = jnp.concatenate(
        [left, first[:, W : S - W], inner, second[:, W : S - W], right], axis=1
    )
    strip = join_rows(strip, region, shares)
    return jnp.stack([strip[:, :S], strip[:, S - W :]])


def on_device(tile_data, tile_counts, modulation, qkv_weight, out_weight, blend_weights):
    h, x, z, yl, _ = where_am_i()
    region = h * 32 + x * 8 + z
    ring = ("h", "yl")

    own_blocks, sent_blocks = packed(qkv_weight.transpose(1, 0, 2), out_weight)
    came_blocks = xor_swap(sent_blocks, "h", 1)

    tile_data, sent_blocks = lax.optimization_barrier((tile_data, sent_blocks))
    away, kept = split_tiles(tile_counts, tile_data)
    came = xor_swap(away, "z", 1)
    came_mod = xor_swap(modulation, "z", 1)

    came_blocks, kept = lax.optimization_barrier((came_blocks, kept))
    straight = yl == h
    out_kept = jnp.where(straight, own_blocks[3:], came_blocks[3:])
    out_sent = jnp.where(straight, came_blocks[3:], own_blocks[3:])
    qkv = jnp.concatenate([own_blocks[:3], came_blocks[:3]])
    qkv, out_sent = lax.optimization_barrier((qkv, out_sent))
    pieces = [xor_swap(qkv, "x", bit) for bit in (1, 2, 3)]
    out_came = xor_swap(out_sent, "yl", 1)
    *pieces, out_came = lax.optimization_barrier((*pieces, out_came))
    block = jnp.concatenate([qkv, *pieces, out_kept, out_came])
    gathered = lax.all_gather(block, "z", axis=0)

    tiles, mods, gate = choose(tile_counts, kept, came, modulation, came_mod)
    mine = tiles.reshape(512, NARROW)
    _, near, across, side = ring_of_four(mine, ring, 0)
    mods_across = xor_swap(mods, "h", 1)
    hid_own = hidden_of((mine, xor_swap(mine, "c", 1), near, xor_swap(near, "c", 1)), mods)
    across, hid_own = lax.optimization_barrier((across, hid_own))
    hid_other = hidden_of(
        (across, xor_swap(across, "c", 1), side, xor_swap(side, "c", 1)), mods_across
    )
    hid_own, hid_other = lax.optimization_barrier((hid_own, hid_other))

    att_sent = attended_of(hid_other, gathered)
    o_block = gathered[:, 24:]
    hid_own, att_sent = lax.optimization_barrier((hid_own, att_sent))
    o_near, o_side = xor_swap(o_block, "x", 1), xor_swap(o_block, "x", 3)
    att_side, att_relay = xor_swap(att_sent, ring, 3), xor_swap(att_sent, ring, 1)
    att_own = attended_of(hid_own, gathered)
    o_near, o_side, att_side, att_relay, att_own = lax.optimization_barrier(
        (o_near, o_side, att_side, att_relay, att_own)
    )
    att_near, att_across = xor_swap(att_own, ring, 1), xor_swap(att_relay, ring, 3)
    o_all = (o_block, o_near, opposite(o_near, o_side, "x", 0), o_side)

    keep, send = partial_of((att_own, att_near, att_across, att_side), o_all)
    summed = keep + xor_swap(send, "c", 1).astype(F32)
    updated = tiles.astype(F32) + gate * summed.reshape(2, TOK, NARROW)
    updated = updated.astype(BF).reshape(2, S, S, NARROW)
    finished = blend(updated, region, blend_weights).reshape(2, TOK, NARROW)
    return place_tiles(tile_counts, finished, xor_swap(finished, "z", 1))


def solution(mesh):
    fine = Mesh(mesh.devices.reshape(2, 4, 8, 2, 2), REGION + MP)
    return jax.shard_map(
        on_device,
        mesh=fine,
        in_specs=(
            P(REGION, None, MP),
            P(),
            P(REGION, None, None),
            P(REGION, None, MP),
            P(REGION, MP),
            P(),
        ),
        out_specs=P(REGION, None, MP),
        check_vma=False,
    )
```

```python
import functools
import math

import jax
import jax.numpy as jnp
from jax import lax
from jax.experimental import pallas as pl
from jax.experimental.pallas import tpu as pltpu
from jax.sharding import Mesh, PartitionSpec as P

D = 2048
HDIM = 128
S = 16
W = 6
TOK = 256
NARROW = 512
HALF = 256
REGION = ("h", "x", "z")
MP = ("yl", "c")
BF = jnp.bfloat16
F32 = jnp.float32


def xor_swap(block, axis, bit):
    size = math.prod(lax.axis_size(a) for a in ((axis,) if isinstance(axis, str) else axis))
    return lax.ppermute(block, axis, [(i, i ^ bit) for i in range(size)])


def rotate(block, axis, step):
    size = lax.axis_size(axis)
    return lax.ppermute(block, axis, [(i, (i + step) % size) for i in range(size)])


def trade(block, distance, lower):
    route = []
    for i in range(64):
        j = i + distance if lower(i) else i - distance
        if 0 <= j < 64:
            route.append((i, j))
    return lax.ppermute(block, REGION, route)


def opposite(near, side, axis, split_axis):
    size = near.shape[split_axis]
    first = xor_swap(lax.slice_in_dim(side, 0, size // 2, axis=split_axis), axis, 1)
    second = xor_swap(lax.slice_in_dim(near, size // 2, size, axis=split_axis), axis, 3)
    return jnp.concatenate([first, second], axis=split_axis)


def ring_of_four(block, axis, split_axis):
    near = xor_swap(block, axis, 1)
    side = xor_swap(block, axis, 3)
    return block, near, opposite(near, side, axis, split_axis), side


def where_am_i():
    h, x, z = (lax.axis_index(a) for a in REGION)
    yl, c = (lax.axis_index(a) for a in MP)
    return h, x, z, yl, c


def even_count(counts_ref):
    h, x, z, _, _ = where_am_i()
    return counts_ref[h * 32 + x * 8 + (z // 2) * 2]


SMEM = pl.BlockSpec(memory_space=pltpu.SMEM)
VMEM = pl.BlockSpec(memory_space=pltpu.VMEM)
HBM = pl.BlockSpec(memory_space=pltpu.HBM)


def cost(flops, size, special=0):
    return pl.CostEstimate(flops=flops, bytes_accessed=size, transcendentals=special)


def pack_kernel(qkv_ref, out_ref, own, sent):
    h = lax.axis_index("h")
    mine = pl.ds(pl.multiple_of(h * HALF, HALF), HALF)
    theirs = pl.ds(pl.multiple_of((1 - h) * HALF, HALF), HALF)
    for n in range(3):
        own[n] = qkv_ref[n, :, mine]
        sent[n] = qkv_ref[n, :, theirs]
    for n in range(2):
        own[3 + n] = out_ref[:, n * HALF : (n + 1) * HALF]
        sent[3 + n] = out_ref[:, n * HALF : (n + 1) * HALF]


def packed(qkv, out):
    return pl.pallas_call(
        pack_kernel,
        in_specs=[VMEM] * 2,
        out_specs=[VMEM] * 2,
        out_shape=[jax.ShapeDtypeStruct((5, 32, HALF), BF)] * 2,
        cost_estimate=cost(0, 2**18),
        compiler_params=pltpu.CompilerParams(vmem_limit_bytes=8 * 2**20),
        name="pack",
    )(qkv, out)


def split_kernel(counts_ref, data_ref, sent_ref, kept_ref, sem):
    even = even_count(counts_ref)
    odd = lax.axis_index("z") % 2 == 1
    copies = []
    for s in range(2):
        away = jnp.where(odd, jnp.clip(s - even, 0, 3), 2 + s)
        stays = jnp.where(odd, jnp.clip(2 + s - even, 0, 3), s)
        copies.append(pltpu.make_async_copy(data_ref.at[away], sent_ref.at[s], sem))
        copies.append(pltpu.make_async_copy(data_ref.at[stays], kept_ref.at[s], sem))
    for copy in copies:
        copy.start()
    for copy in copies:
        copy.wait()


def split_tiles(counts, data):
    return pl.pallas_call(
        split_kernel,
        in_specs=[SMEM, HBM],
        out_specs=[VMEM, VMEM],
        out_shape=[jax.ShapeDtypeStruct((2, TOK, NARROW), BF)] * 2,
        scratch_shapes=[pltpu.SemaphoreType.DMA],
        cost_estimate=cost(0, 2**21),
        compiler_params=pltpu.CompilerParams(vmem_limit_bytes=12 * 2**20),
        name="split",
    )(counts, data)


def choose_kernel(counts_ref, kept, came, mod, other_mod, tiles, mods, gate):
    even = even_count(counts_ref)
    odd = lax.axis_index("z") % 2 == 1
    place = lax.axis_index("yl") * 2 + lax.axis_index("c")
    cols = pl.ds(pl.multiple_of(place * NARROW, NARROW), NARROW)
    for s in range(2):
        use_other = jnp.where(odd, 2 + s < even, s >= even)

        @pl.when(use_other)
        def _():
            tiles[s] = came[s]
            mods[s] = other_mod[0]
            gate[s] = other_mod[0, 2:3, cols].astype(F32)

        @pl.when(jnp.logical_not(use_other))
        def _():
            tiles[s] = kept[s]
            mods[s] = mod[0]
            gate[s] = mod[0, 2:3, cols].astype(F32)


def choose(counts, kept, came, mod, other_mod):
    return pl.pallas_call(
        choose_kernel,
        in_specs=[SMEM] + [VMEM] * 4,
        out_specs=[VMEM] * 3,
        out_shape=[
            jax.ShapeDtypeStruct((2, TOK, NARROW), BF),
            jax.ShapeDtypeStruct((2, 3, D), BF),
            jax.ShapeDtypeStruct((2, 1, NARROW), F32),
        ],
        cost_estimate=cost(0, 2**21),
        compiler_params=pltpu.CompilerParams(vmem_limit_bytes=12 * 2**20),
        name="choose",
    )(counts, kept, came, mod, other_mod)


def hidden_kernel(a_ref, b_ref, c_ref, d_ref, mod_ref, out_ref):
    place = lax.axis_index("yl") * 2 + lax.axis_index("c")
    parts = [r[...].astype(F32) for r in (a_ref, b_ref, c_ref, d_ref)]
    mean = sum(jnp.sum(p, axis=-1, keepdims=True) for p in parts) * (1.0 / D)
    parts = [p - mean for p in parts]
    spread = sum(jnp.sum(p * p, axis=-1, keepdims=True) for p in parts) * (1.0 / D)
    scale = lax.rsqrt(spread + 1e-06)
    for j, p in enumerate(parts):
        source = pl.ds(pl.multiple_of((place ^ j) * NARROW, NARROW), NARROW)
        gain = 1.0 + mod_ref[0, 1:2, source].astype(F32)
        value = p * scale * gain + mod_ref[0, 0:1, source].astype(F32)
        out_ref[:, j * NARROW : (j + 1) * NARROW] = value.astype(BF)


def hidden_of(pieces, mods):
    rows = 256
    piece = pl.BlockSpec((rows, NARROW), lambda i: (i, 0))
    return pl.pallas_call(
        hidden_kernel,
        grid=(512 // rows,),
        in_specs=[piece] * 4 + [pl.BlockSpec((1, 3, D), lambda i: (i * rows // TOK, 0, 0))],
        out_specs=pl.BlockSpec((rows, D), lambda i: (i, 0)),
        out_shape=jax.ShapeDtypeStruct((512, D), BF),
        cost_estimate=cost(8 * 512 * D, 4 * 512 * D, 512),
        compiler_params=pltpu.CompilerParams(vmem_limit_bytes=24 * 2**20),
        name="hidden",
    )(*pieces, mods)


def attend_kernel(hid_hbm, g_ref, out_ref, hid_ref, w_ref, total_ref, sem):
    h, x, _, yl, c = where_am_i()
    copies = []
    for j in range(4):
        cols = pl.ds(j * NARROW, NARROW)
        group = [pltpu.make_async_copy(hid_hbm.at[:, cols], hid_ref.at[:, cols], sem.at[j])]
        hr = (yl ^ (j // 2)) ^ h
        for half in range(2):
            xr = ((c ^ (j % 2)) * 2 + half) ^ x
            for n in range(3):
                group.append(
                    pltpu.make_async_copy(
                        g_ref.at[:, (xr * 2 + hr) * 3 + n],
                        w_ref.at[j, half, :, :, pl.ds(n * HALF, HALF)],
                        sem.at[j],
                    )
                )
        for copy in group:
            copy.start()
        copies.append(group)
    for j, group in enumerate(copies):
        for copy in group:
            copy.wait()
        part = jnp.dot(
            hid_ref[:, j * NARROW : (j + 1) * NARROW],
            w_ref[j].reshape(NARROW, 3 * HALF),
            preferred_element_type=F32,
        )
        if j == 0:
            total_ref[...] = part
        elif j < 3:
            total_ref[...] += part
    proj = (total_ref[...] + part).astype(BF)

    def block(t, kind, n):
        start = kind * HALF + n * HDIM
        return proj[t * TOK : (t + 1) * TOK, start : start + HDIM]

    units = [(t, n) for t in range(2) for n in range(2)]
    scores = [
        lax.dot_general(
            block(t, 0, n), block(t, 1, n), (((1,), (1,)), ((), ())), preferred_element_type=F32
        )
        * (1.0 / math.sqrt(HDIM))
        for t, n in units
    ]
    exps = [jnp.exp(s - jnp.max(s, axis=-1, keepdims=True)) for s in scores]
    for e, (t, n) in zip(exps, units):
        got = jnp.dot(e.astype(BF), block(t, 2, n), preferred_element_type=F32)
        got = got / jnp.sum(e, axis=-1, keepdims=True)
        out_ref[t * TOK : (t + 1) * TOK, n * HDIM : (n + 1) * HDIM] = got.astype(BF)


def attended_of(hidden, gathered):
    return pl.pallas_call(
        attend_kernel,
        in_specs=[HBM] * 2,
        out_specs=VMEM,
        out_shape=jax.ShapeDtypeStruct((512, HALF), BF),
        scratch_shapes=[
            pltpu.VMEM((512, D), BF),
            pltpu.VMEM((4, 2, 8, 32, 3 * HALF), BF),
            pltpu.VMEM((512, 3 * HALF), F32),
            pltpu.SemaphoreType.DMA((4,)),
        ],
        compiler_params=pltpu.CompilerParams(vmem_limit_bytes=60 * 2**20),
        cost_estimate=cost(
            2 * (2 * 512 * D * 768 + 4 * 4 * TOK * TOK * HDIM), 6 * 2**20, 4 * TOK * TOK
        ),
        name="attend",
    )(hidden, gathered)


def project_kernel(a_ref, b_ref, c_ref, d_ref, o0, o1, o2, o3, keep_ref, send_ref, w_ref, sem):
    h, x, _, _, c = where_am_i()
    copies = []
    for xr, piece in enumerate((o0, o1, o2, o3)):
        px = x ^ xr
        slot = ((px // 2) ^ c) * 2 + px % 2
        for j in range(4):
            block = (j % 2) * 2 + (h ^ (j // 2))
            copies.append(
                pltpu.make_async_copy(
                    piece.at[:, block], w_ref.at[slot, :, :, pl.ds(j * HALF, HALF)], sem
                )
            )
    for copy in copies:
        copy.start()
    for copy in copies:
        copy.wait()
    attended = jnp.concatenate([r[...] for r in (a_ref, b_ref, c_ref, d_ref)], axis=1)
    for b, out_ref in ((1, send_ref), (0, keep_ref)):
        weight = w_ref[2 * b : 2 * b + 2].reshape(NARROW, 4 * HALF)
        total = lax.dot_general(
            attended, weight, (((1,), (1,)), ((), ())), preferred_element_type=F32
        )
        out_ref[...] = total.astype(out_ref.dtype)


def partial_of(attended, os):
    return pl.pallas_call(
        project_kernel,
        in_specs=[VMEM] * 4 + [HBM] * 4,
        out_specs=[VMEM] * 2,
        out_shape=[
            jax.ShapeDtypeStruct((512, NARROW), F32),
            jax.ShapeDtypeStruct((512, NARROW), BF),
        ],
        scratch_shapes=[pltpu.VMEM((4, 8, 32, 4 * HALF), BF), pltpu.SemaphoreType.DMA],
        compiler_params=pltpu.CompilerParams(vmem_limit_bytes=16 * 2**20),
        cost_estimate=cost(2 * 512 * 1024 * 1024, 4 * 2**20),
        name="project",
    )(*attended, *os)


def place_kernel(counts_ref, tiles_ref, out_ref, zero_ref, sem):
    even = even_count(counts_ref)
    parity = lax.axis_index("z") % 2
    zero_ref[...] = jnp.zeros_like(zero_ref)
    waits = []
    for slot in range(4):
        tile = slot + parity * even
        live = jnp.where(parity == 1, tile < 4, slot < even)
        target = out_ref.at[slot]

        @pl.when(live)
        def _():
            pltpu.make_async_copy(tiles_ref.at[jnp.minimum(tile, 3)], target, sem).start()

        @pl.when(jnp.logical_not(live))
        def _():
            pltpu.make_async_copy(zero_ref, target, sem).start()

        waits.append(pltpu.make_async_copy(zero_ref, target, sem))
    for wait in waits:
        wait.wait()


def place_tiles(counts, tiles):
    return pl.pallas_call(
        place_kernel,
        in_specs=[SMEM, VMEM],
        out_specs=HBM,
        out_shape=jax.ShapeDtypeStruct((4, TOK, NARROW), BF),
        scratch_shapes=[pltpu.VMEM((TOK, NARROW), BF), pltpu.SemaphoreType.DMA],
        cost_estimate=cost(0, 2**21),
        compiler_params=pltpu.CompilerParams(vmem_limit_bytes=12 * 2**20),
        name="place",
    )(counts, tiles)


def mix(earlier, later, share):
    return ((1.0 - share) * earlier.astype(F32) + share * later.astype(F32)).astype(BF)


def join_rows(strip, region, shares):
    count = strip.shape[1]
    share = shares.reshape(W, 1, 1)
    top, bottom = strip[:W], strip[S - W :]
    north, south = top.reshape(W * count, NARROW), bottom.reshape(W * count, NARROW)
    first = region % 8 < 4
    same = trade(jnp.where(first, south, north), 4, lambda i: i % 8 < 4)
    cross = trade(jnp.where(first, north, south), 4, lambda i: i % 8 >= 4)
    same, cross = lax.optimization_barrier((same, cross))
    later, earlier = jnp.where(first, same, cross), jnp.where(first, cross, same)
    top = jnp.where(region >= 4, mix(earlier.reshape(W, count, NARROW), top, share), top)
    bottom = jnp.where(region < 60, mix(bottom, later.reshape(W, count, NARROW), share), bottom)
    return jnp.concatenate([top, strip[W : S - W], bottom], axis=0)


def join_tiles(tiles, region, shares):
    first, second = tiles[0], tiles[1]
    inner = mix(first[:, S - W :], second[:, :W], shares.reshape(1, W, 1))
    strip = jnp.concatenate([first[:, : S - W], inner, second[:, W:]], axis=1)
    return join_rows(strip, region, shares)


def join_pair(own, other, edge, region, shares):
    share = shares.reshape(1, W, 1)
    odd = region % 2 == 1
    low, high = jnp.where(odd, other, own), jnp.where(odd, own, other)
    west, east = low[:, :W], high[:, -W:]
    front = region % 4 < 2
    west = jnp.where(front, west, mix(edge, west, share))
    east = jnp.where(front, mix(east, edge, share), east)
    middle = mix(low[:, -W:], high[:, :W], share)
    n = 2 * S - W
    return jnp.stack(
        [
            jnp.concatenate([west, low[:, W:S]], axis=1),
            jnp.concatenate([low[:, S - W : n - W], middle], axis=1),
            jnp.concatenate([middle, high[:, W:S]], axis=1),
            jnp.concatenate([high[:, S - W : n - W], east], axis=1),
        ]
    )


def on_device(tile_data, tile_counts, modulation, qkv_weight, out_weight, blend_weights):
    h, x, z, yl, _ = where_am_i()
    region = h * 32 + x * 8 + z
    ring = ("h", "yl")

    own_blocks, sent_blocks = packed(qkv_weight.transpose(1, 0, 2), out_weight)
    came_blocks = xor_swap(sent_blocks, "h", 1)

    tile_data, sent_blocks = lax.optimization_barrier((tile_data, sent_blocks))
    away, kept = split_tiles(tile_counts, tile_data)
    came = xor_swap(away, "z", 1)
    came_mod = xor_swap(modulation, "z", 1)

    came_blocks, kept = lax.optimization_barrier((came_blocks, kept))
    straight = yl == h
    out_kept = jnp.where(straight, own_blocks[3:], came_blocks[3:])
    out_sent = jnp.where(straight, came_blocks[3:], own_blocks[3:])
    qkv = jnp.concatenate([own_blocks[:3], came_blocks[:3]])
    qkv, out_sent = lax.optimization_barrier((qkv, out_sent))
    pieces = [xor_swap(qkv, "x", bit) for bit in (1, 2, 3)]
    out_came = xor_swap(out_sent, "yl", 1)
    *pieces, out_came = lax.optimization_barrier((*pieces, out_came))
    block = jnp.concatenate([qkv, *pieces, out_kept, out_came])
    gathered = lax.all_gather(block, "z", axis=0)

    tiles, mods, gate = choose(tile_counts, kept, came, modulation, came_mod)
    mine = tiles.reshape(512, NARROW)
    _, near, across, side = ring_of_four(mine, ring, 0)
    mods_across = xor_swap(mods, "h", 1)
    hid_own = hidden_of((mine, xor_swap(mine, "c", 1), near, xor_swap(near, "c", 1)), mods)
    across, hid_own = lax.optimization_barrier((across, hid_own))
    hid_other = hidden_of(
        (across, xor_swap(across, "c", 1), side, xor_swap(side, "c", 1)), mods_across
    )
    hid_own, hid_other = lax.optimization_barrier((hid_own, hid_other))

    att_sent = attended_of(hid_other, gathered)
    o_block = gathered[:, 24:]
    hid_own, att_sent = lax.optimization_barrier((hid_own, att_sent))
    o_near, o_side = xor_swap(o_block, "x", 1), xor_swap(o_block, "x", 3)
    att_side, att_relay = xor_swap(att_sent, ring, 3), xor_swap(att_sent, ring, 1)
    att_own = attended_of(hid_own, gathered)
    o_near, o_side, att_side, att_relay, att_own = lax.optimization_barrier(
        (o_near, o_side, att_side, att_relay, att_own)
    )
    att_near, att_across = xor_swap(att_own, ring, 1), xor_swap(att_relay, ring, 3)
    o_all = (o_block, o_near, opposite(o_near, o_side, "x", 0), o_side)

    keep, send = partial_of((att_own, att_near, att_across, att_side), o_all)
    summed = keep + xor_swap(send, "c", 1).astype(F32)
    updated = tiles.astype(F32) + gate * summed.reshape(2, TOK, NARROW)
    updated = updated.astype(BF).reshape(2, S, S, NARROW)
    strip = join_tiles(updated, region, blend_weights)

    edge = jnp.where(region % 4 == 1, strip[:, -W:], strip[:, :W]).reshape(S * W, NARROW)
    beside = lax.ppermute(
        edge, REGION, [(i, i ^ 3) for i in range(64) if i % 4 in (1, 2)]
    )
    beyond = lax.ppermute(
        edge, REGION, [(i, i ^ 2) for i in range(64) if i % 4 in (1, 2)]
    )
    other = xor_swap(strip.reshape(-1, NARROW), "z", 1)
    other, beside, beyond = lax.optimization_barrier((other, beside, beyond))
    edge = jnp.where((region % 4 == 1) | (region % 4 == 2), beside, beyond).reshape(S, W, NARROW)
    joined = join_pair(strip, other.reshape(strip.shape), edge, region, blend_weights)
    return place_tiles(tile_counts, joined.reshape(4, TOK, NARROW))


def solution(mesh):
    fine = Mesh(mesh.devices.reshape(2, 4, 8, 2, 2), REGION + MP)
    return jax.shard_map(
        on_device,
        mesh=fine,
        in_specs=(
            P(REGION, None, MP),
            P(),
            P(REGION, None, None),
            P(REGION, None, MP),
            P(REGION, MP),
            P(),
        ),
        out_specs=P(REGION, None, MP),
        check_vma=False,
    )
```

```python
import functools
import math

import jax
import jax.numpy as jnp
from jax import lax
from jax.experimental import pallas as pl
from jax.experimental.pallas import tpu as pltpu
from jax.sharding import Mesh, PartitionSpec as P

D = 2048
HDIM = 128
S = 16
W = 6
TOK = 256
NARROW = 512
HALF = 256
REGION = ("h", "x", "z")
MP = ("yl", "c")
BF = jnp.bfloat16
F32 = jnp.float32


def xor_swap(block, axis, bit):
    size = math.prod(lax.axis_size(a) for a in ((axis,) if isinstance(axis, str) else axis))
    return lax.ppermute(block, axis, [(i, i ^ bit) for i in range(size)])


def rotate(block, axis, step):
    size = lax.axis_size(axis)
    return lax.ppermute(block, axis, [(i, (i + step) % size) for i in range(size)])


def trade(block, distance, lower):
    route = []
    for i in range(64):
        j = i + distance if lower(i) else i - distance
        if 0 <= j < 64:
            route.append((i, j))
    return lax.ppermute(block, REGION, route)


def opposite(near, side, axis, split_axis):
    size = near.shape[split_axis]
    first = xor_swap(lax.slice_in_dim(side, 0, size // 2, axis=split_axis), axis, 1)
    second = xor_swap(lax.slice_in_dim(near, size // 2, size, axis=split_axis), axis, 3)
    return jnp.concatenate([first, second], axis=split_axis)


def ring_of_four(block, axis, split_axis):
    near = xor_swap(block, axis, 1)
    side = xor_swap(block, axis, 3)
    return block, near, opposite(near, side, axis, split_axis), side


def where_am_i():
    h, x, z = (lax.axis_index(a) for a in REGION)
    yl, c = (lax.axis_index(a) for a in MP)
    return h, x, z, yl, c


def even_count(counts_ref):
    h, x, z, _, _ = where_am_i()
    return counts_ref[h * 32 + x * 8 + (z // 2) * 2]


SMEM = pl.BlockSpec(memory_space=pltpu.SMEM)
VMEM = pl.BlockSpec(memory_space=pltpu.VMEM)
HBM = pl.BlockSpec(memory_space=pltpu.HBM)


def cost(flops, size, special=0):
    return pl.CostEstimate(flops=flops, bytes_accessed=size, transcendentals=special)


def pack_kernel(qkv_ref, out_ref, own, sent):
    h = lax.axis_index("h")
    mine = pl.ds(pl.multiple_of(h * HALF, HALF), HALF)
    theirs = pl.ds(pl.multiple_of((1 - h) * HALF, HALF), HALF)
    for n in range(3):
        own[n] = qkv_ref[n, :, mine]
        sent[n] = qkv_ref[n, :, theirs]
    for n in range(2):
        own[3 + n] = out_ref[:, n * HALF : (n + 1) * HALF]
        sent[3 + n] = out_ref[:, n * HALF : (n + 1) * HALF]


def packed(qkv, out):
    return pl.pallas_call(
        pack_kernel,
        in_specs=[VMEM] * 2,
        out_specs=[VMEM] * 2,
        out_shape=[jax.ShapeDtypeStruct((5, 32, HALF), BF)] * 2,
        cost_estimate=cost(0, 2**18),
        compiler_params=pltpu.CompilerParams(vmem_limit_bytes=8 * 2**20),
        name="pack",
    )(qkv, out)


def split_kernel(counts_ref, data_ref, sent_ref, kept_ref, sem):
    even = even_count(counts_ref)
    odd = lax.axis_index("z") % 2 == 1
    copies = []
    for s in range(2):
        away = jnp.where(odd, jnp.clip(s - even, 0, 3), 2 + s)
        stays = jnp.where(odd, jnp.clip(2 + s - even, 0, 3), s)
        copies.append(pltpu.make_async_copy(data_ref.at[away], sent_ref.at[s], sem))
        copies.append(pltpu.make_async_copy(data_ref.at[stays], kept_ref.at[s], sem))
    for copy in copies:
        copy.start()
    for copy in copies:
        copy.wait()


def split_tiles(counts, data):
    return pl.pallas_call(
        split_kernel,
        in_specs=[SMEM, HBM],
        out_specs=[VMEM, VMEM],
        out_shape=[jax.ShapeDtypeStruct((2, TOK, NARROW), BF)] * 2,
        scratch_shapes=[pltpu.SemaphoreType.DMA],
        cost_estimate=cost(0, 2**21),
        compiler_params=pltpu.CompilerParams(vmem_limit_bytes=12 * 2**20),
        name="split",
    )(counts, data)


def choose_kernel(counts_ref, kept, came, mod, other_mod, tiles, mods, gate):
    even = even_count(counts_ref)
    odd = lax.axis_index("z") % 2 == 1
    place = lax.axis_index("yl") * 2 + lax.axis_index("c")
    cols = pl.ds(pl.multiple_of(place * NARROW, NARROW), NARROW)
    for s in range(2):
        use_other = jnp.where(odd, 2 + s < even, s >= even)

        @pl.when(use_other)
        def _():
            tiles[s] = came[s]
            mods[s] = other_mod[0]
            gate[s] = other_mod[0, 2:3, cols].astype(F32)

        @pl.when(jnp.logical_not(use_other))
        def _():
            tiles[s] = kept[s]
            mods[s] = mod[0]
            gate[s] = mod[0, 2:3, cols].astype(F32)


def choose(counts, kept, came, mod, other_mod):
    return pl.pallas_call(
        choose_kernel,
        in_specs=[SMEM] + [VMEM] * 4,
        out_specs=[VMEM] * 3,
        out_shape=[
            jax.ShapeDtypeStruct((2, TOK, NARROW), BF),
            jax.ShapeDtypeStruct((2, 3, D), BF),
            jax.ShapeDtypeStruct((2, 1, NARROW), F32),
        ],
        cost_estimate=cost(0, 2**21),
        compiler_params=pltpu.CompilerParams(vmem_limit_bytes=12 * 2**20),
        name="choose",
    )(counts, kept, came, mod, other_mod)


def hidden_kernel(a_ref, b_ref, c_ref, d_ref, mod_ref, out_ref):
    place = lax.axis_index("yl") * 2 + lax.axis_index("c")
    parts = [r[...].astype(F32) for r in (a_ref, b_ref, c_ref, d_ref)]
    mean = sum(jnp.sum(p, axis=-1, keepdims=True) for p in parts) * (1.0 / D)
    parts = [p - mean for p in parts]
    spread = sum(jnp.sum(p * p, axis=-1, keepdims=True) for p in parts) * (1.0 / D)
    scale = lax.rsqrt(spread + 1e-06)
    for j, p in enumerate(parts):
        source = pl.ds(pl.multiple_of((place ^ j) * NARROW, NARROW), NARROW)
        gain = 1.0 + mod_ref[0, 1:2, source].astype(F32)
        value = p * scale * gain + mod_ref[0, 0:1, source].astype(F32)
        out_ref[:, j * NARROW : (j + 1) * NARROW] = value.astype(BF)


def hidden_of(pieces, mods):
    rows = 256
    piece = pl.BlockSpec((rows, NARROW), lambda i: (i, 0))
    return pl.pallas_call(
        hidden_kernel,
        grid=(512 // rows,),
        in_specs=[piece] * 4 + [pl.BlockSpec((1, 3, D), lambda i: (i * rows // TOK, 0, 0))],
        out_specs=pl.BlockSpec((rows, D), lambda i: (i, 0)),
        out_shape=jax.ShapeDtypeStruct((512, D), BF),
        cost_estimate=cost(8 * 512 * D, 4 * 512 * D, 512),
        compiler_params=pltpu.CompilerParams(vmem_limit_bytes=24 * 2**20),
        name="hidden",
    )(*pieces, mods)


def attend_kernel(hid_hbm, g_ref, out_ref, hid_ref, w_ref, total_ref, sem):
    h, x, _, yl, c = where_am_i()
    copies = []
    for j in range(4):
        cols = pl.ds(j * NARROW, NARROW)
        group = [pltpu.make_async_copy(hid_hbm.at[:, cols], hid_ref.at[:, cols], sem.at[j])]
        hr = (yl ^ (j // 2)) ^ h
        for half in range(2):
            xr = ((c ^ (j % 2)) * 2 + half) ^ x
            for n in range(3):
                group.append(
                    pltpu.make_async_copy(
                        g_ref.at[:, (xr * 2 + hr) * 3 + n],
                        w_ref.at[j, half, :, :, pl.ds(n * HALF, HALF)],
                        sem.at[j],
                    )
                )
        for copy in group:
            copy.start()
        copies.append(group)
    for j, group in enumerate(copies):
        for copy in group:
            copy.wait()
        part = jnp.dot(
            hid_ref[:, j * NARROW : (j + 1) * NARROW],
            w_ref[j].reshape(NARROW, 3 * HALF),
            preferred_element_type=F32,
        )
        if j == 0:
            total_ref[...] = part
        elif j < 3:
            total_ref[...] += part
    proj = (total_ref[...] + part).astype(BF)

    def block(t, kind, n):
        start = kind * HALF + n * HDIM
        return proj[t * TOK : (t + 1) * TOK, start : start + HDIM]

    units = [(t, n) for t in range(2) for n in range(2)]
    scores = [
        lax.dot_general(
            block(t, 0, n), block(t, 1, n), (((1,), (1,)), ((), ())), preferred_element_type=F32
        )
        * (1.0 / math.sqrt(HDIM))
        for t, n in units
    ]
    exps = [jnp.exp(s - jnp.max(s, axis=-1, keepdims=True)) for s in scores]
    for e, (t, n) in zip(exps, units):
        got = jnp.dot(e.astype(BF), block(t, 2, n), preferred_element_type=F32)
        got = got / jnp.sum(e, axis=-1, keepdims=True)
        out_ref[t * TOK : (t + 1) * TOK, n * HDIM : (n + 1) * HDIM] = got.astype(BF)


def attended_of(hidden, gathered):
    return pl.pallas_call(
        attend_kernel,
        in_specs=[HBM] * 2,
        out_specs=VMEM,
        out_shape=jax.ShapeDtypeStruct((512, HALF), BF),
        scratch_shapes=[
            pltpu.VMEM((512, D), BF),
            pltpu.VMEM((4, 2, 8, 32, 3 * HALF), BF),
            pltpu.VMEM((512, 3 * HALF), F32),
            pltpu.SemaphoreType.DMA((4,)),
        ],
        compiler_params=pltpu.CompilerParams(vmem_limit_bytes=60 * 2**20),
        cost_estimate=cost(
            2 * (2 * 512 * D * 768 + 4 * 4 * TOK * TOK * HDIM), 6 * 2**20, 4 * TOK * TOK
        ),
        name="attend",
    )(hidden, gathered)


def project_kernel(a_ref, b_ref, c_ref, d_ref, o0, o1, o2, o3, keep_ref, send_ref, w_ref, sem):
    h, x, _, _, c = where_am_i()
    copies = []
    for xr, piece in enumerate((o0, o1, o2, o3)):
        px = x ^ xr
        slot = ((px // 2) ^ c) * 2 + px % 2
        for j in range(4):
            block = (j % 2) * 2 + (h ^ (j // 2))
            copies.append(
                pltpu.make_async_copy(
                    piece.at[:, block], w_ref.at[slot, :, :, pl.ds(j * HALF, HALF)], sem
                )
            )
    for copy in copies:
        copy.start()
    for copy in copies:
        copy.wait()
    attended = jnp.concatenate([r[...] for r in (a_ref, b_ref, c_ref, d_ref)], axis=1)
    for b, out_ref in ((1, send_ref), (0, keep_ref)):
        weight = w_ref[2 * b : 2 * b + 2].reshape(NARROW, 4 * HALF)
        total = lax.dot_general(
            attended, weight, (((1,), (1,)), ((), ())), preferred_element_type=F32
        )
        out_ref[...] = total.astype(out_ref.dtype)


def partial_of(attended, os):
    return pl.pallas_call(
        project_kernel,
        in_specs=[VMEM] * 4 + [HBM] * 4,
        out_specs=[VMEM] * 2,
        out_shape=[
            jax.ShapeDtypeStruct((512, NARROW), F32),
            jax.ShapeDtypeStruct((512, NARROW), BF),
        ],
        scratch_shapes=[pltpu.VMEM((4, 8, 32, 4 * HALF), BF), pltpu.SemaphoreType.DMA],
        compiler_params=pltpu.CompilerParams(vmem_limit_bytes=16 * 2**20),
        cost_estimate=cost(2 * 512 * 1024 * 1024, 4 * 2**20),
        name="project",
    )(*attended, *os)


def place_kernel(counts_ref, tiles_ref, out_ref, zero_ref, sem):
    even = even_count(counts_ref)
    parity = lax.axis_index("z") % 2
    zero_ref[...] = jnp.zeros_like(zero_ref)
    waits = []
    for slot in range(4):
        tile = slot + parity * even
        live = jnp.where(parity == 1, tile < 4, slot < even)
        target = out_ref.at[slot]

        @pl.when(live)
        def _():
            pltpu.make_async_copy(tiles_ref.at[jnp.minimum(tile, 3)], target, sem).start()

        @pl.when(jnp.logical_not(live))
        def _():
            pltpu.make_async_copy(zero_ref, target, sem).start()

        waits.append(pltpu.make_async_copy(zero_ref, target, sem))
    for wait in waits:
        wait.wait()


def place_tiles(counts, tiles):
    return pl.pallas_call(
        place_kernel,
        in_specs=[SMEM, VMEM],
        out_specs=HBM,
        out_shape=jax.ShapeDtypeStruct((4, TOK, NARROW), BF),
        scratch_shapes=[pltpu.VMEM((TOK, NARROW), BF), pltpu.SemaphoreType.DMA],
        cost_estimate=cost(0, 2**21),
        compiler_params=pltpu.CompilerParams(vmem_limit_bytes=12 * 2**20),
        name="place",
    )(counts, tiles)


def mix(earlier, later, share):
    return ((1.0 - share) * earlier.astype(F32) + share * later.astype(F32)).astype(BF)


def join_rows(strip, region, shares):
    count = strip.shape[1]
    share = shares.reshape(W, 1, 1)
    top, bottom = strip[:W], strip[S - W :]
    north, south = top.reshape(W * count, NARROW), bottom.reshape(W * count, NARROW)
    first = region % 8 < 4
    cross = trade(jnp.where(first, north, south), 4, lambda i: i % 8 >= 4)
    same = trade(jnp.where(first, south, north), 4, lambda i: i % 8 < 4)
    cross, same = lax.optimization_barrier((cross, same))
    later, earlier = jnp.where(first, same, cross), jnp.where(first, cross, same)
    top = jnp.where(region >= 4, mix(earlier.reshape(W, count, NARROW), top, share), top)
    bottom = jnp.where(region < 60, mix(bottom, later.reshape(W, count, NARROW), share), bottom)
    return jnp.concatenate([top, strip[W : S - W], bottom], axis=0)


def join_tiles(tiles, region, shares):
    first, second = tiles[0], tiles[1]
    inner = mix(first[:, S - W :], second[:, :W], shares.reshape(1, W, 1))
    strip = jnp.concatenate([first[:, : S - W], inner, second[:, W:]], axis=1)
    return join_rows(strip, region, shares)


def join_pair(own, other, edge, region, shares):
    share = shares.reshape(1, W, 1)
    odd = region % 2 == 1
    low, high = jnp.where(odd, other, own), jnp.where(odd, own, other)
    west, east = low[:, :W], high[:, -W:]
    front = region % 4 < 2
    west = jnp.where(front, west, mix(edge, west, share))
    east = jnp.where(front, mix(east, edge, share), east)
    middle = mix(low[:, -W:], high[:, :W], share)
    n = 2 * S - W
    return jnp.stack(
        [
            jnp.concatenate([west, low[:, W:S]], axis=1),
            jnp.concatenate([low[:, S - W : n - W], middle], axis=1),
            jnp.concatenate([middle, high[:, W:S]], axis=1),
            jnp.concatenate([high[:, S - W : n - W], east], axis=1),
        ]
    )


def on_device(tile_data, tile_counts, modulation, qkv_weight, out_weight, blend_weights):
    h, x, z, yl, _ = where_am_i()
    region = h * 32 + x * 8 + z
    ring = ("h", "yl")

    own_blocks, sent_blocks = packed(qkv_weight.transpose(1, 0, 2), out_weight)
    came_blocks = xor_swap(sent_blocks, "h", 1)

    tile_data, sent_blocks = lax.optimization_barrier((tile_data, sent_blocks))
    away, kept = split_tiles(tile_counts, tile_data)
    came = xor_swap(away, "z", 1)
    came_mod = xor_swap(modulation, "z", 1)

    came_blocks, kept = lax.optimization_barrier((came_blocks, kept))
    straight = yl == h
    out_kept = jnp.where(straight, own_blocks[3:], came_blocks[3:])
    out_sent = jnp.where(straight, came_blocks[3:], own_blocks[3:])
    qkv = jnp.concatenate([own_blocks[:3], came_blocks[:3]])
    qkv, out_sent = lax.optimization_barrier((qkv, out_sent))
    x_far, x_near, x_side = (xor_swap(qkv, "x", bit) for bit in (2, 1, 3))
    out_came = xor_swap(out_sent, "yl", 1)
    x_far, x_near, x_side, out_came = lax.optimization_barrier((x_far, x_near, x_side, out_came))
    block = jnp.concatenate([qkv, x_near, x_far, x_side, out_kept, out_came])
    gathered = lax.all_gather(block, "z", axis=0)

    tiles, mods, gate = choose(tile_counts, kept, came, modulation, came_mod)
    mine = tiles.reshape(512, NARROW)
    _, near, across, side = ring_of_four(mine, ring, 0)
    mods_across = xor_swap(mods, "h", 1)
    hid_own = hidden_of((mine, xor_swap(mine, "c", 1), near, xor_swap(near, "c", 1)), mods)
    across, hid_own = lax.optimization_barrier((across, hid_own))
    hid_other = hidden_of(
        (across, xor_swap(across, "c", 1), side, xor_swap(side, "c", 1)), mods_across
    )
    hid_own, hid_other = lax.optimization_barrier((hid_own, hid_other))

    att_sent = attended_of(hid_other, gathered)
    o_block = gathered[:, 24:]
    hid_own, att_sent = lax.optimization_barrier((hid_own, att_sent))
    o_near, o_side = xor_swap(o_block, "x", 1), xor_swap(o_block, "x", 3)
    att_side, att_relay = xor_swap(att_sent, ring, 3), xor_swap(att_sent, ring, 1)
    att_own = attended_of(hid_own, gathered)
    o_near, o_side, att_side, att_relay, att_own = lax.optimization_barrier(
        (o_near, o_side, att_side, att_relay, att_own)
    )
    att_near, att_across = xor_swap(att_own, ring, 1), xor_swap(att_relay, ring, 3)
    o_all = (o_block, o_near, opposite(o_near, o_side, "x", 0), o_side)

    keep, send = partial_of((att_own, att_near, att_across, att_side), o_all)
    summed = keep + xor_swap(send, "c", 1).astype(F32)
    updated = tiles.astype(F32) + gate * summed.reshape(2, TOK, NARROW)
    updated = updated.astype(BF).reshape(2, S, S, NARROW)
    strip = join_tiles(updated, region, blend_weights)

    other = xor_swap(strip.reshape(-1, NARROW), "z", 1)
    edge = jnp.where(region % 4 == 1, strip[:, -W:], strip[:, :W]).reshape(S * W, NARROW)
    beside = lax.ppermute(
        edge, REGION, [(i, i ^ 3) for i in range(64) if i % 4 in (1, 2)]
    )
    beyond = lax.ppermute(
        edge, REGION, [(i, i ^ 2) for i in range(64) if i % 4 in (1, 2)]
    )
    beside, beyond, other = lax.optimization_barrier((beside, beyond, other))
    edge = jnp.where((region % 4 == 1) | (region % 4 == 2), beside, beyond).reshape(S, W, NARROW)
    joined = join_pair(strip, other.reshape(strip.shape), edge, region, blend_weights)
    return place_tiles(tile_counts, joined.reshape(4, TOK, NARROW))


def solution(mesh):
    fine = Mesh(mesh.devices.reshape(2, 4, 8, 2, 2), REGION + MP)
    return jax.shard_map(
        on_device,
        mesh=fine,
        in_specs=(
            P(REGION, None, MP),
            P(),
            P(REGION, None, None),
            P(REGION, None, MP),
            P(REGION, MP),
            P(),
        ),
        out_specs=P(REGION, None, MP),
        check_vma=False,
    )
```

```python
import functools
import math

import jax
import jax.numpy as jnp
from jax import lax
from jax.experimental import pallas as pl
from jax.experimental.pallas import tpu as pltpu
from jax.sharding import Mesh, PartitionSpec as P

D = 2048
HDIM = 128
S = 16
W = 6
TOK = 256
NARROW = 512
HALF = 256
REGION = ("h", "x", "z")
MP = ("yl", "c")
BF = jnp.bfloat16
F32 = jnp.float32


def xor_swap(block, axis, bit):
    size = math.prod(lax.axis_size(a) for a in ((axis,) if isinstance(axis, str) else axis))
    return lax.ppermute(block, axis, [(i, i ^ bit) for i in range(size)])


def rotate(block, axis, step):
    size = lax.axis_size(axis)
    return lax.ppermute(block, axis, [(i, (i + step) % size) for i in range(size)])


def trade(block, distance, lower):
    route = []
    for i in range(64):
        j = i + distance if lower(i) else i - distance
        if 0 <= j < 64:
            route.append((i, j))
    return lax.ppermute(block, REGION, route)


def opposite(near, side, axis, split_axis):
    size = near.shape[split_axis]
    first = xor_swap(lax.slice_in_dim(side, 0, size // 2, axis=split_axis), axis, 1)
    second = xor_swap(lax.slice_in_dim(near, size // 2, size, axis=split_axis), axis, 3)
    return jnp.concatenate([first, second], axis=split_axis)


def ring_of_four(block, axis, split_axis):
    near = xor_swap(block, axis, 1)
    side = xor_swap(block, axis, 3)
    return block, near, opposite(near, side, axis, split_axis), side


def where_am_i():
    h, x, z = (lax.axis_index(a) for a in REGION)
    yl, c = (lax.axis_index(a) for a in MP)
    return h, x, z, yl, c


def even_count(counts_ref):
    h, x, z, _, _ = where_am_i()
    return counts_ref[h * 32 + x * 8 + (z // 2) * 2]


SMEM = pl.BlockSpec(memory_space=pltpu.SMEM)
VMEM = pl.BlockSpec(memory_space=pltpu.VMEM)
HBM = pl.BlockSpec(memory_space=pltpu.HBM)


def cost(flops, size, special=0):
    return pl.CostEstimate(flops=flops, bytes_accessed=size, transcendentals=special)


def pack_kernel(qkv_ref, out_ref, own, sent):
    h = lax.axis_index("h")
    mine = pl.ds(pl.multiple_of(h * HALF, HALF), HALF)
    theirs = pl.ds(pl.multiple_of((1 - h) * HALF, HALF), HALF)
    for n in range(3):
        own[n] = qkv_ref[n, :, mine]
        sent[n] = qkv_ref[n, :, theirs]
    for n in range(2):
        own[3 + n] = out_ref[:, n * HALF : (n + 1) * HALF]
        sent[3 + n] = out_ref[:, n * HALF : (n + 1) * HALF]


def packed(qkv, out):
    return pl.pallas_call(
        pack_kernel,
        in_specs=[VMEM] * 2,
        out_specs=[VMEM] * 2,
        out_shape=[jax.ShapeDtypeStruct((5, 32, HALF), BF)] * 2,
        cost_estimate=cost(0, 2**18),
        compiler_params=pltpu.CompilerParams(vmem_limit_bytes=8 * 2**20),
        name="pack",
    )(qkv, out)


def split_kernel(counts_ref, data_ref, sent_ref, kept_ref, sem):
    even = even_count(counts_ref)
    odd = lax.axis_index("z") % 2 == 1
    copies = []
    for s in range(2):
        away = jnp.where(odd, jnp.clip(s - even, 0, 3), 2 + s)
        stays = jnp.where(odd, jnp.clip(2 + s - even, 0, 3), s)
        copies.append(pltpu.make_async_copy(data_ref.at[away], sent_ref.at[s], sem))
        copies.append(pltpu.make_async_copy(data_ref.at[stays], kept_ref.at[s], sem))
    for copy in copies:
        copy.start()
    for copy in copies:
        copy.wait()


def split_tiles(counts, data):
    return pl.pallas_call(
        split_kernel,
        in_specs=[SMEM, HBM],
        out_specs=[VMEM, VMEM],
        out_shape=[jax.ShapeDtypeStruct((2, TOK, NARROW), BF)] * 2,
        scratch_shapes=[pltpu.SemaphoreType.DMA],
        cost_estimate=cost(0, 2**21),
        compiler_params=pltpu.CompilerParams(vmem_limit_bytes=12 * 2**20),
        name="split",
    )(counts, data)


def choose_kernel(counts_ref, kept, came, mod, other_mod, tiles, mods, gate):
    even = even_count(counts_ref)
    odd = lax.axis_index("z") % 2 == 1
    place = lax.axis_index("yl") * 2 + lax.axis_index("c")
    cols = pl.ds(pl.multiple_of(place * NARROW, NARROW), NARROW)
    for s in range(2):
        use_other = jnp.where(odd, 2 + s < even, s >= even)

        @pl.when(use_other)
        def _():
            tiles[s] = came[s]
            mods[s] = other_mod[0]
            gate[s] = other_mod[0, 2:3, cols].astype(F32)

        @pl.when(jnp.logical_not(use_other))
        def _():
            tiles[s] = kept[s]
            mods[s] = mod[0]
            gate[s] = mod[0, 2:3, cols].astype(F32)


def choose(counts, kept, came, mod, other_mod):
    return pl.pallas_call(
        choose_kernel,
        in_specs=[SMEM] + [VMEM] * 4,
        out_specs=[VMEM] * 3,
        out_shape=[
            jax.ShapeDtypeStruct((2, TOK, NARROW), BF),
            jax.ShapeDtypeStruct((2, 3, D), BF),
            jax.ShapeDtypeStruct((2, 1, NARROW), F32),
        ],
        cost_estimate=cost(0, 2**21),
        compiler_params=pltpu.CompilerParams(vmem_limit_bytes=12 * 2**20),
        name="choose",
    )(counts, kept, came, mod, other_mod)


def hidden_kernel(a_ref, b_ref, c_ref, d_ref, mod_ref, out_ref):
    place = lax.axis_index("yl") * 2 + lax.axis_index("c")
    parts = [r[...].astype(F32) for r in (a_ref, b_ref, c_ref, d_ref)]
    mean = sum(jnp.sum(p, axis=-1, keepdims=True) for p in parts) * (1.0 / D)
    parts = [p - mean for p in parts]
    spread = sum(jnp.sum(p * p, axis=-1, keepdims=True) for p in parts) * (1.0 / D)
    scale = lax.rsqrt(spread + 1e-06)
    for j, p in enumerate(parts):
        source = pl.ds(pl.multiple_of((place ^ j) * NARROW, NARROW), NARROW)
        gain = 1.0 + mod_ref[0, 1:2, source].astype(F32)
        value = p * scale * gain + mod_ref[0, 0:1, source].astype(F32)
        out_ref[:, j * NARROW : (j + 1) * NARROW] = value.astype(BF)


def hidden_of(pieces, mods):
    rows = 256
    piece = pl.BlockSpec((rows, NARROW), lambda i: (i, 0))
    return pl.pallas_call(
        hidden_kernel,
        grid=(512 // rows,),
        in_specs=[piece] * 4 + [pl.BlockSpec((1, 3, D), lambda i: (i * rows // TOK, 0, 0))],
        out_specs=pl.BlockSpec((rows, D), lambda i: (i, 0)),
        out_shape=jax.ShapeDtypeStruct((512, D), BF),
        cost_estimate=cost(8 * 512 * D, 4 * 512 * D, 512),
        compiler_params=pltpu.CompilerParams(vmem_limit_bytes=24 * 2**20),
        name="hidden",
    )(*pieces, mods)


def attend_kernel(hid_hbm, g_ref, out_ref, hid_ref, w_ref, total_ref, sem):
    h, x, _, yl, c = where_am_i()
    copies = []
    for j in range(4):
        cols = pl.ds(j * NARROW, NARROW)
        group = [pltpu.make_async_copy(hid_hbm.at[:, cols], hid_ref.at[:, cols], sem.at[j])]
        hr = (yl ^ (j // 2)) ^ h
        for half in range(2):
            xr = ((c ^ (j % 2)) * 2 + half) ^ x
            for n in range(3):
                group.append(
                    pltpu.make_async_copy(
                        g_ref.at[:, (xr * 2 + hr) * 3 + n],
                        w_ref.at[j, half, :, :, pl.ds(n * HALF, HALF)],
                        sem.at[j],
                    )
                )
        for copy in group:
            copy.start()
        copies.append(group)
    for j, group in enumerate(copies):
        for copy in group:
            copy.wait()
        part = jnp.dot(
            hid_ref[:, j * NARROW : (j + 1) * NARROW],
            w_ref[j].reshape(NARROW, 3 * HALF),
            preferred_element_type=F32,
        )
        if j == 0:
            total_ref[...] = part
        elif j < 3:
            total_ref[...] += part
    proj = (total_ref[...] + part).astype(BF)

    def block(t, kind, n):
        start = kind * HALF + n * HDIM
        return proj[t * TOK : (t + 1) * TOK, start : start + HDIM]

    units = [(t, n) for t in range(2) for n in range(2)]
    scores = [
        lax.dot_general(
            block(t, 0, n), block(t, 1, n), (((1,), (1,)), ((), ())), preferred_element_type=F32
        )
        * (1.0 / math.sqrt(HDIM))
        for t, n in units
    ]
    exps = [jnp.exp(s - jnp.max(s, axis=-1, keepdims=True)) for s in scores]
    for e, (t, n) in zip(exps, units):
        got = jnp.dot(e.astype(BF), block(t, 2, n), preferred_element_type=F32)
        got = got / jnp.sum(e, axis=-1, keepdims=True)
        out_ref[t * TOK : (t + 1) * TOK, n * HDIM : (n + 1) * HDIM] = got.astype(BF)


def attended_of(hidden, gathered):
    return pl.pallas_call(
        attend_kernel,
        in_specs=[HBM] * 2,
        out_specs=VMEM,
        out_shape=jax.ShapeDtypeStruct((512, HALF), BF),
        scratch_shapes=[
            pltpu.VMEM((512, D), BF),
            pltpu.VMEM((4, 2, 8, 32, 3 * HALF), BF),
            pltpu.VMEM((512, 3 * HALF), F32),
            pltpu.SemaphoreType.DMA((4,)),
        ],
        compiler_params=pltpu.CompilerParams(vmem_limit_bytes=60 * 2**20),
        cost_estimate=cost(
            2 * (2 * 512 * D * 768 + 4 * 4 * TOK * TOK * HDIM), 6 * 2**20, 4 * TOK * TOK
        ),
        name="attend",
    )(hidden, gathered)


def project_kernel(a_ref, b_ref, c_ref, d_ref, o0, o1, o2, o3, keep_ref, send_ref, w_ref, sem):
    h, x, _, _, c = where_am_i()
    copies = []
    for xr, piece in enumerate((o0, o1, o2, o3)):
        px = x ^ xr
        slot = ((px // 2) ^ c) * 2 + px % 2
        for j in range(4):
            block = (j % 2) * 2 + (h ^ (j // 2))
            copies.append(
                pltpu.make_async_copy(
                    piece.at[:, block], w_ref.at[slot, :, :, pl.ds(j * HALF, HALF)], sem
                )
            )
    for copy in copies:
        copy.start()
    for copy in copies:
        copy.wait()
    attended = jnp.concatenate([r[...] for r in (a_ref, b_ref, c_ref, d_ref)], axis=1)
    for b, out_ref in ((1, send_ref), (0, keep_ref)):
        weight = w_ref[2 * b : 2 * b + 2].reshape(NARROW, 4 * HALF)
        total = lax.dot_general(
            attended, weight, (((1,), (1,)), ((), ())), preferred_element_type=F32
        )
        out_ref[...] = total.astype(out_ref.dtype)


def partial_of(attended, os):
    return pl.pallas_call(
        project_kernel,
        in_specs=[VMEM] * 4 + [HBM] * 4,
        out_specs=[VMEM] * 2,
        out_shape=[
            jax.ShapeDtypeStruct((512, NARROW), F32),
            jax.ShapeDtypeStruct((512, NARROW), BF),
        ],
        scratch_shapes=[pltpu.VMEM((4, 8, 32, 4 * HALF), BF), pltpu.SemaphoreType.DMA],
        compiler_params=pltpu.CompilerParams(vmem_limit_bytes=16 * 2**20),
        cost_estimate=cost(2 * 512 * 1024 * 1024, 4 * 2**20),
        name="project",
    )(*attended, *os)


def place_kernel(counts_ref, tiles_ref, out_ref, zero_ref, sem):
    even = even_count(counts_ref)
    parity = lax.axis_index("z") % 2
    zero_ref[...] = jnp.zeros_like(zero_ref)
    waits = []
    for slot in range(4):
        tile = slot + parity * even
        live = jnp.where(parity == 1, tile < 4, slot < even)
        target = out_ref.at[slot]

        @pl.when(live)
        def _():
            pltpu.make_async_copy(tiles_ref.at[jnp.minimum(tile, 3)], target, sem).start()

        @pl.when(jnp.logical_not(live))
        def _():
            pltpu.make_async_copy(zero_ref, target, sem).start()

        waits.append(pltpu.make_async_copy(zero_ref, target, sem))
    for wait in waits:
        wait.wait()


def place_tiles(counts, tiles):
    return pl.pallas_call(
        place_kernel,
        in_specs=[SMEM, VMEM],
        out_specs=HBM,
        out_shape=jax.ShapeDtypeStruct((4, TOK, NARROW), BF),
        scratch_shapes=[pltpu.VMEM((TOK, NARROW), BF), pltpu.SemaphoreType.DMA],
        cost_estimate=cost(0, 2**21),
        compiler_params=pltpu.CompilerParams(vmem_limit_bytes=12 * 2**20),
        name="place",
    )(counts, tiles)


def mix(earlier, later, share):
    return ((1.0 - share) * earlier.astype(F32) + share * later.astype(F32)).astype(BF)


def join_rows(strip, region, shares):
    count = strip.shape[1]
    share = shares.reshape(W, 1, 1)
    top, bottom = strip[:W], strip[S - W :]
    north, south = top.reshape(W * count, NARROW), bottom.reshape(W * count, NARROW)
    first = region % 8 < 4
    cross = trade(jnp.where(first, north, south), 4, lambda i: i % 8 >= 4)
    same = trade(jnp.where(first, south, north), 4, lambda i: i % 8 < 4)
    cross, same = lax.optimization_barrier((cross, same))
    later, earlier = jnp.where(first, same, cross), jnp.where(first, cross, same)
    top = jnp.where(region >= 4, mix(earlier.reshape(W, count, NARROW), top, share), top)
    bottom = jnp.where(region < 60, mix(bottom, later.reshape(W, count, NARROW), share), bottom)
    return jnp.concatenate([top, strip[W : S - W], bottom], axis=0)


def join_tiles(tiles, region, shares):
    first, second = tiles[0], tiles[1]
    inner = mix(first[:, S - W :], second[:, :W], shares.reshape(1, W, 1))
    strip = jnp.concatenate([first[:, : S - W], inner, second[:, W:]], axis=1)
    return join_rows(strip, region, shares)


def join_pair(own, other, edge, region, shares):
    share = shares.reshape(1, W, 1)
    odd = region % 2 == 1
    low, high = jnp.where(odd, other, own), jnp.where(odd, own, other)
    west, east = low[:, :W], high[:, -W:]
    front = region % 4 < 2
    west = jnp.where(front, west, mix(edge, west, share))
    east = jnp.where(front, mix(east, edge, share), east)
    middle = mix(low[:, -W:], high[:, :W], share)
    n = 2 * S - W
    return jnp.stack(
        [
            jnp.concatenate([west, low[:, W:S]], axis=1),
            jnp.concatenate([low[:, S - W : n - W], middle], axis=1),
            jnp.concatenate([middle, high[:, W:S]], axis=1),
            jnp.concatenate([high[:, S - W : n - W], east], axis=1),
        ]
    )


def on_device(tile_data, tile_counts, modulation, qkv_weight, out_weight, blend_weights):
    h, x, z, yl, _ = where_am_i()
    region = h * 32 + x * 8 + z
    ring = ("h", "yl")

    own_blocks, sent_blocks = packed(qkv_weight.transpose(1, 0, 2), out_weight)
    came_blocks = xor_swap(sent_blocks, "h", 1)

    tile_data, sent_blocks = lax.optimization_barrier((tile_data, sent_blocks))
    away, kept = split_tiles(tile_counts, tile_data)
    came = xor_swap(away, "z", 1)
    came_mod = xor_swap(modulation, "z", 1)

    came_blocks, kept = lax.optimization_barrier((came_blocks, kept))
    straight = yl == h
    out_kept = jnp.where(straight, own_blocks[3:], came_blocks[3:])
    out_sent = jnp.where(straight, came_blocks[3:], own_blocks[3:])
    qkv = jnp.concatenate([own_blocks[:3], came_blocks[:3]])
    qkv, out_sent = lax.optimization_barrier((qkv, out_sent))
    x_far, x_near, x_side = (xor_swap(qkv, "x", bit) for bit in (2, 1, 3))
    out_came = xor_swap(out_sent, "yl", 1)
    x_far, x_near, x_side, out_came = lax.optimization_barrier((x_far, x_near, x_side, out_came))
    block = jnp.concatenate([qkv, x_near, x_far, x_side, out_kept, out_came])
    gathered = lax.all_gather(block, "z", axis=0)

    tiles, mods, gate = choose(tile_counts, kept, came, modulation, came_mod)
    mine = tiles.reshape(512, NARROW)
    _, near, across, side = ring_of_four(mine, ring, 0)
    mods_across = xor_swap(mods, "h", 1)
    hid_own = hidden_of((mine, xor_swap(mine, "c", 1), near, xor_swap(near, "c", 1)), mods)
    across, hid_own, mods_across = lax.optimization_barrier((across, hid_own, mods_across))
    hid_other = hidden_of(
        (across, xor_swap(across, "c", 1), side, xor_swap(side, "c", 1)), mods_across
    )
    hid_own, hid_other = lax.optimization_barrier((hid_own, hid_other))

    att_sent = attended_of(hid_other, gathered)
    o_block = gathered[:, 24:]
    hid_own, att_sent = lax.optimization_barrier((hid_own, att_sent))
    o_near, o_side = xor_swap(o_block, "x", 1), xor_swap(o_block, "x", 3)
    att_side, att_relay = xor_swap(att_sent, ring, 3), xor_swap(att_sent, ring, 1)
    att_own = attended_of(hid_own, gathered)
    o_near, o_side, att_side, att_relay, att_own = lax.optimization_barrier(
        (o_near, o_side, att_side, att_relay, att_own)
    )
    att_near, att_across = xor_swap(att_own, ring, 1), xor_swap(att_relay, ring, 3)
    o_all = (o_block, o_near, opposite(o_near, o_side, "x", 0), o_side)

    keep, send = partial_of((att_own, att_near, att_across, att_side), o_all)
    summed = keep + xor_swap(send, "c", 1).astype(F32)
    updated = tiles.astype(F32) + gate * summed.reshape(2, TOK, NARROW)
    updated = updated.astype(BF).reshape(2, S, S, NARROW)
    strip = join_tiles(updated, region, blend_weights)

    other = xor_swap(strip.reshape(-1, NARROW), "z", 1)
    edge = jnp.where(region % 4 == 1, strip[:, -W:], strip[:, :W]).reshape(S * W, NARROW)
    beside = lax.ppermute(
        edge, REGION, [(i, i ^ 3) for i in range(64) if i % 4 in (1, 2)]
    )
    beyond = lax.ppermute(
        edge, REGION, [(i, i ^ 2) for i in range(64) if i % 4 in (1, 2)]
    )
    other, beside, beyond = lax.optimization_barrier((other, beside, beyond))
    edge = jnp.where((region % 4 == 1) | (region % 4 == 2), beside, beyond).reshape(S, W, NARROW)
    joined = join_pair(strip, other.reshape(strip.shape), edge, region, blend_weights)
    return place_tiles(tile_counts, joined.reshape(4, TOK, NARROW))


def solution(mesh):
    fine = Mesh(mesh.devices.reshape(2, 4, 8, 2, 2), REGION + MP)
    return jax.shard_map(
        on_device,
        mesh=fine,
        in_specs=(
            P(REGION, None, MP),
            P(),
            P(REGION, None, None),
            P(REGION, None, MP),
            P(REGION, MP),
            P(),
        ),
        out_specs=P(REGION, None, MP),
        check_vma=False,
    )
```

```python
import functools
import math

import jax
import jax.numpy as jnp
from jax import lax
from jax.experimental import pallas as pl
from jax.experimental.pallas import tpu as pltpu
from jax.sharding import Mesh, PartitionSpec as P

D = 2048
HDIM = 128
S = 16
W = 6
TOK = 256
NARROW = 512
HALF = 256
REGION = ("h", "x", "z")
MP = ("yl", "c")
BF = jnp.bfloat16
F32 = jnp.float32


def xor_swap(block, axis, bit):
    size = math.prod(lax.axis_size(a) for a in ((axis,) if isinstance(axis, str) else axis))
    return lax.ppermute(block, axis, [(i, i ^ bit) for i in range(size)])


def rotate(block, axis, step):
    size = lax.axis_size(axis)
    return lax.ppermute(block, axis, [(i, (i + step) % size) for i in range(size)])


def trade(block, distance, lower):
    route = []
    for i in range(64):
        j = i + distance if lower(i) else i - distance
        if 0 <= j < 64:
            route.append((i, j))
    return lax.ppermute(block, REGION, route)


def opposite(near, side, axis, split_axis):
    size = near.shape[split_axis]
    first = xor_swap(lax.slice_in_dim(side, 0, size // 2, axis=split_axis), axis, 1)
    second = xor_swap(lax.slice_in_dim(near, size // 2, size, axis=split_axis), axis, 3)
    return jnp.concatenate([first, second], axis=split_axis)


def ring_of_four(block, axis, split_axis):
    near = xor_swap(block, axis, 1)
    side = xor_swap(block, axis, 3)
    return block, near, opposite(near, side, axis, split_axis), side


def where_am_i():
    h, x, z = (lax.axis_index(a) for a in REGION)
    yl, c = (lax.axis_index(a) for a in MP)
    return h, x, z, yl, c


def even_count(counts_ref):
    h, x, z, _, _ = where_am_i()
    return counts_ref[h * 32 + x * 8 + (z // 2) * 2]


SMEM = pl.BlockSpec(memory_space=pltpu.SMEM)
VMEM = pl.BlockSpec(memory_space=pltpu.VMEM)
HBM = pl.BlockSpec(memory_space=pltpu.HBM)


def cost(flops, size, special=0):
    return pl.CostEstimate(flops=flops, bytes_accessed=size, transcendentals=special)


def pack_kernel(qkv_ref, out_ref, own, sent):
    h = lax.axis_index("h")
    mine = pl.ds(pl.multiple_of(h * HALF, HALF), HALF)
    theirs = pl.ds(pl.multiple_of((1 - h) * HALF, HALF), HALF)
    for n in range(3):
        own[n] = qkv_ref[n, :, mine]
        sent[n] = qkv_ref[n, :, theirs]
    for n in range(2):
        own[3 + n] = out_ref[:, n * HALF : (n + 1) * HALF]
        sent[3 + n] = out_ref[:, n * HALF : (n + 1) * HALF]


def packed(qkv, out):
    return pl.pallas_call(
        pack_kernel,
        in_specs=[VMEM] * 2,
        out_specs=[VMEM] * 2,
        out_shape=[jax.ShapeDtypeStruct((5, 32, HALF), BF)] * 2,
        cost_estimate=cost(0, 2**18),
        compiler_params=pltpu.CompilerParams(vmem_limit_bytes=8 * 2**20),
        name="pack",
    )(qkv, out)


def split_kernel(counts_ref, data_ref, sent_ref, kept_ref, sem):
    even = even_count(counts_ref)
    odd = lax.axis_index("z") % 2 == 1
    copies = []
    for s in range(2):
        away = jnp.where(odd, jnp.clip(s - even, 0, 3), 2 + s)
        stays = jnp.where(odd, jnp.clip(2 + s - even, 0, 3), s)
        copies.append(pltpu.make_async_copy(data_ref.at[away], sent_ref.at[s], sem))
        copies.append(pltpu.make_async_copy(data_ref.at[stays], kept_ref.at[s], sem))
    for copy in copies:
        copy.start()
    for copy in copies:
        copy.wait()


def split_tiles(counts, data):
    return pl.pallas_call(
        split_kernel,
        in_specs=[SMEM, HBM],
        out_specs=[VMEM, VMEM],
        out_shape=[jax.ShapeDtypeStruct((2, TOK, NARROW), BF)] * 2,
        scratch_shapes=[pltpu.SemaphoreType.DMA],
        cost_estimate=cost(0, 2**21),
        compiler_params=pltpu.CompilerParams(vmem_limit_bytes=12 * 2**20),
        name="split",
    )(counts, data)


def choose_kernel(counts_ref, kept, came, mod, other_mod, tiles, mods, gate):
    even = even_count(counts_ref)
    odd = lax.axis_index("z") % 2 == 1
    place = lax.axis_index("yl") * 2 + lax.axis_index("c")
    cols = pl.ds(pl.multiple_of(place * NARROW, NARROW), NARROW)
    for s in range(2):
        use_other = jnp.where(odd, 2 + s < even, s >= even)

        @pl.when(use_other)
        def _():
            tiles[s] = came[s]
            mods[s] = other_mod[0]
            gate[s] = other_mod[0, 2:3, cols].astype(F32)

        @pl.when(jnp.logical_not(use_other))
        def _():
            tiles[s] = kept[s]
            mods[s] = mod[0]
            gate[s] = mod[0, 2:3, cols].astype(F32)


def choose(counts, kept, came, mod, other_mod):
    return pl.pallas_call(
        choose_kernel,
        in_specs=[SMEM] + [VMEM] * 4,
        out_specs=[VMEM] * 3,
        out_shape=[
            jax.ShapeDtypeStruct((2, TOK, NARROW), BF),
            jax.ShapeDtypeStruct((2, 3, D), BF),
            jax.ShapeDtypeStruct((2, 1, NARROW), F32),
        ],
        cost_estimate=cost(0, 2**21),
        compiler_params=pltpu.CompilerParams(vmem_limit_bytes=12 * 2**20),
        name="choose",
    )(counts, kept, came, mod, other_mod)


def hidden_kernel(a_ref, b_ref, c_ref, d_ref, mod_ref, out_ref):
    place = lax.axis_index("yl") * 2 + lax.axis_index("c")
    parts = [r[...].astype(F32) for r in (a_ref, b_ref, c_ref, d_ref)]
    mean = sum(jnp.sum(p, axis=-1, keepdims=True) for p in parts) * (1.0 / D)
    parts = [p - mean for p in parts]
    spread = sum(jnp.sum(p * p, axis=-1, keepdims=True) for p in parts) * (1.0 / D)
    scale = lax.rsqrt(spread + 1e-06)
    for j, p in enumerate(parts):
        source = pl.ds(pl.multiple_of((place ^ j) * NARROW, NARROW), NARROW)
        gain = 1.0 + mod_ref[0, 1:2, source].astype(F32)
        value = p * scale * gain + mod_ref[0, 0:1, source].astype(F32)
        out_ref[:, j * NARROW : (j + 1) * NARROW] = value.astype(BF)


def hidden_of(pieces, mods):
    rows = 256
    piece = pl.BlockSpec((rows, NARROW), lambda i: (i, 0))
    return pl.pallas_call(
        hidden_kernel,
        grid=(512 // rows,),
        in_specs=[piece] * 4 + [pl.BlockSpec((1, 3, D), lambda i: (i * rows // TOK, 0, 0))],
        out_specs=pl.BlockSpec((rows, D), lambda i: (i, 0)),
        out_shape=jax.ShapeDtypeStruct((512, D), BF),
        cost_estimate=cost(8 * 512 * D, 4 * 512 * D, 512),
        compiler_params=pltpu.CompilerParams(vmem_limit_bytes=24 * 2**20),
        name="hidden",
    )(*pieces, mods)


def attend_kernel(hid_hbm, g_ref, out_ref, hid_ref, w_ref, total_ref, sem):
    h, x, _, yl, c = where_am_i()
    copies = []
    for j in range(4):
        cols = pl.ds(j * NARROW, NARROW)
        group = [pltpu.make_async_copy(hid_hbm.at[:, cols], hid_ref.at[:, cols], sem.at[j])]
        hr = (yl ^ (j // 2)) ^ h
        for half in range(2):
            xr = ((c ^ (j % 2)) * 2 + half) ^ x
            for n in range(3):
                group.append(
                    pltpu.make_async_copy(
                        g_ref.at[:, (xr * 2 + hr) * 3 + n],
                        w_ref.at[j, half, :, :, pl.ds(n * HALF, HALF)],
                        sem.at[j],
                    )
                )
        for copy in group:
            copy.start()
        copies.append(group)
    for j, group in enumerate(copies):
        for copy in group:
            copy.wait()
        part = jnp.dot(
            hid_ref[:, j * NARROW : (j + 1) * NARROW],
            w_ref[j].reshape(NARROW, 3 * HALF),
            preferred_element_type=F32,
        )
        if j == 0:
            total_ref[...] = part
        elif j < 3:
            total_ref[...] += part
    proj = (total_ref[...] + part).astype(BF)

    def block(t, kind, n):
        start = kind * HALF + n * HDIM
        return proj[t * TOK : (t + 1) * TOK, start : start + HDIM]

    units = [(t, n) for t in range(2) for n in range(2)]
    scores = [
        lax.dot_general(
            block(t, 0, n), block(t, 1, n), (((1,), (1,)), ((), ())), preferred_element_type=F32
        )
        * (1.0 / math.sqrt(HDIM))
        for t, n in units
    ]
    exps = [jnp.exp(s - jnp.max(s, axis=-1, keepdims=True)) for s in scores]
    for e, (t, n) in zip(exps, units):
        got = jnp.dot(e.astype(BF), block(t, 2, n), preferred_element_type=F32)
        got = got / jnp.sum(e, axis=-1, keepdims=True)
        out_ref[t * TOK : (t + 1) * TOK, n * HDIM : (n + 1) * HDIM] = got.astype(BF)


def attended_of(hidden, gathered):
    return pl.pallas_call(
        attend_kernel,
        in_specs=[HBM] * 2,
        out_specs=VMEM,
        out_shape=jax.ShapeDtypeStruct((512, HALF), BF),
        scratch_shapes=[
            pltpu.VMEM((512, D), BF),
            pltpu.VMEM((4, 2, 8, 32, 3 * HALF), BF),
            pltpu.VMEM((512, 3 * HALF), F32),
            pltpu.SemaphoreType.DMA((4,)),
        ],
        compiler_params=pltpu.CompilerParams(vmem_limit_bytes=60 * 2**20),
        cost_estimate=cost(
            2 * (2 * 512 * D * 768 + 4 * 4 * TOK * TOK * HDIM), 6 * 2**20, 4 * TOK * TOK
        ),
        name="attend",
    )(hidden, gathered)


def project_kernel(far, a_ref, b_ref, c_ref, d_ref, o0, o1, o2, o3, out_ref, w_ref, sem):
    h, x, _, _, c = where_am_i()
    first = ((x // 2) ^ c) == far
    waits = []
    for k in range(2):
        for pair, use in (((o0, o1), first), ((o2, o3), jnp.logical_not(first))):

            @pl.when(use)
            def _():
                for j in range(4):
                    block = (j % 2) * 2 + (h ^ (j // 2))
                    pltpu.make_async_copy(
                        pair[k].at[:, block], w_ref.at[(x ^ k) % 2, :, :, pl.ds(j * HALF, HALF)], sem
                    ).start()

        for j in range(4):
            waits.append(
                pltpu.make_async_copy(
                    o0.at[:, j], w_ref.at[(x ^ k) % 2, :, :, pl.ds(j * HALF, HALF)], sem
                )
            )
    for wait in waits:
        wait.wait()
    attended = jnp.concatenate([r[...] for r in (a_ref, b_ref, c_ref, d_ref)], axis=1)
    weight = w_ref[...].reshape(NARROW, 4 * HALF)
    total = lax.dot_general(
        attended, weight, (((1,), (1,)), ((), ())), preferred_element_type=F32
    )
    out_ref[...] = total.astype(out_ref.dtype)


def partial_of(far, attended, os):
    return pl.pallas_call(
        functools.partial(project_kernel, far),
        in_specs=[VMEM] * 4 + [HBM] * 4,
        out_specs=VMEM,
        out_shape=jax.ShapeDtypeStruct((512, NARROW), BF if far else F32),
        scratch_shapes=[pltpu.VMEM((2, 8, 32, 4 * HALF), BF), pltpu.SemaphoreType.DMA],
        compiler_params=pltpu.CompilerParams(vmem_limit_bytes=16 * 2**20),
        cost_estimate=cost(512 * 1024 * 1024, 2 * 2**20),
        name="project",
    )(*attended, *os)


def place_kernel(counts_ref, tiles_ref, out_ref, zero_ref, sem):
    even = even_count(counts_ref)
    parity = lax.axis_index("z") % 2
    zero_ref[...] = jnp.zeros_like(zero_ref)
    waits = []
    for slot in range(4):
        tile = slot + parity * even
        live = jnp.where(parity == 1, tile < 4, slot < even)
        target = out_ref.at[slot]

        @pl.when(live)
        def _():
            pltpu.make_async_copy(tiles_ref.at[jnp.minimum(tile, 3)], target, sem).start()

        @pl.when(jnp.logical_not(live))
        def _():
            pltpu.make_async_copy(zero_ref, target, sem).start()

        waits.append(pltpu.make_async_copy(zero_ref, target, sem))
    for wait in waits:
        wait.wait()


def place_tiles(counts, tiles):
    return pl.pallas_call(
        place_kernel,
        in_specs=[SMEM, VMEM],
        out_specs=HBM,
        out_shape=jax.ShapeDtypeStruct((4, TOK, NARROW), BF),
        scratch_shapes=[pltpu.VMEM((TOK, NARROW), BF), pltpu.SemaphoreType.DMA],
        cost_estimate=cost(0, 2**21),
        compiler_params=pltpu.CompilerParams(vmem_limit_bytes=12 * 2**20),
        name="place",
    )(counts, tiles)


def mix(earlier, later, share):
    return ((1.0 - share) * earlier.astype(F32) + share * later.astype(F32)).astype(BF)


def join_rows(strip, region, shares):
    count = strip.shape[1]
    share = shares.reshape(W, 1, 1)
    top, bottom = strip[:W], strip[S - W :]
    north, south = top.reshape(W * count, NARROW), bottom.reshape(W * count, NARROW)
    first = region % 8 < 4
    cross = trade(jnp.where(first, north, south), 4, lambda i: i % 8 >= 4)
    same = trade(jnp.where(first, south, north), 4, lambda i: i % 8 < 4)
    cross, same = lax.optimization_barrier((cross, same))
    later, earlier = jnp.where(first, same, cross), jnp.where(first, cross, same)
    top = jnp.where(region >= 4, mix(earlier.reshape(W, count, NARROW), top, share), top)
    bottom = jnp.where(region < 60, mix(bottom, later.reshape(W, count, NARROW), share), bottom)
    return jnp.concatenate([top, strip[W : S - W], bottom], axis=0)


def join_tiles(tiles, region, shares):
    first, second = tiles[0], tiles[1]
    inner = mix(first[:, S - W :], second[:, :W], shares.reshape(1, W, 1))
    strip = jnp.concatenate([first[:, : S - W], inner, second[:, W:]], axis=1)
    return join_rows(strip, region, shares)


def join_pair(own, other, edge, region, shares):
    share = shares.reshape(1, W, 1)
    odd = region % 2 == 1
    low, high = jnp.where(odd, other, own), jnp.where(odd, own, other)
    west, east = low[:, :W], high[:, -W:]
    front = region % 4 < 2
    west = jnp.where(front, west, mix(edge, west, share))
    east = jnp.where(front, mix(east, edge, share), east)
    middle = mix(low[:, -W:], high[:, :W], share)
    n = 2 * S - W
    return jnp.stack(
        [
            jnp.concatenate([west, low[:, W:S]], axis=1),
            jnp.concatenate([low[:, S - W : n - W], middle], axis=1),
            jnp.concatenate([middle, high[:, W:S]], axis=1),
            jnp.concatenate([high[:, S - W : n - W], east], axis=1),
        ]
    )


def on_device(tile_data, tile_counts, modulation, qkv_weight, out_weight, blend_weights):
    h, x, z, yl, _ = where_am_i()
    region = h * 32 + x * 8 + z
    ring = ("h", "yl")

    own_blocks, sent_blocks = packed(qkv_weight.transpose(1, 0, 2), out_weight)
    came_blocks = xor_swap(sent_blocks, "h", 1)

    tile_data, sent_blocks = lax.optimization_barrier((tile_data, sent_blocks))
    away, kept = split_tiles(tile_counts, tile_data)
    came = xor_swap(away, "z", 1)
    came_mod = xor_swap(modulation, "z", 1)

    came_blocks, kept = lax.optimization_barrier((came_blocks, kept))
    straight = yl == h
    out_kept = jnp.where(straight, own_blocks[3:], came_blocks[3:])
    out_sent = jnp.where(straight, came_blocks[3:], own_blocks[3:])
    qkv = jnp.concatenate([own_blocks[:3], came_blocks[:3]])
    qkv, out_sent = lax.optimization_barrier((qkv, out_sent))
    x_far, x_near, x_side = (xor_swap(qkv, "x", bit) for bit in (2, 1, 3))
    out_came = xor_swap(out_sent, "yl", 1)
    x_far, x_near, x_side, out_came = lax.optimization_barrier((x_far, x_near, x_side, out_came))
    block = jnp.concatenate([qkv, x_near, x_far, x_side, out_kept, out_came])
    gathered = lax.all_gather(block, "z", axis=0)

    tiles, mods, gate = choose(tile_counts, kept, came, modulation, came_mod)
    mine = tiles.reshape(512, NARROW)
    _, near, across, side = ring_of_four(mine, ring, 0)
    mods_across = xor_swap(mods, "h", 1)
    hid_own = hidden_of((mine, xor_swap(mine, "c", 1), near, xor_swap(near, "c", 1)), mods)
    across, hid_own, mods_across = lax.optimization_barrier((across, hid_own, mods_across))
    hid_other = hidden_of(
        (across, xor_swap(across, "c", 1), side, xor_swap(side, "c", 1)), mods_across
    )
    hid_own, hid_other = lax.optimization_barrier((hid_own, hid_other))

    att_sent = attended_of(hid_other, gathered)
    o_block = gathered[:, 24:]
    hid_own, att_sent = lax.optimization_barrier((hid_own, att_sent))
    o_near, o_side = xor_swap(o_block, "x", 1), xor_swap(o_block, "x", 3)
    att_side, att_relay = xor_swap(att_sent, ring, 3), xor_swap(att_sent, ring, 1)
    att_own = attended_of(hid_own, gathered)
    o_near, o_side, att_side, att_relay, att_own = lax.optimization_barrier(
        (o_near, o_side, att_side, att_relay, att_own)
    )
    att_near, att_across = xor_swap(att_own, ring, 1), xor_swap(att_relay, ring, 3)
    o_all = (o_block, o_near, opposite(o_near, o_side, "x", 0), o_side)

    attended = (att_own, att_near, att_across, att_side)
    send = partial_of(1, attended, o_all)
    summed = partial_of(0, attended, o_all) + xor_swap(send, "c", 1).astype(F32)
    updated = tiles.astype(F32) + gate * summed.reshape(2, TOK, NARROW)
    updated = updated.astype(BF).reshape(2, S, S, NARROW)
    strip = join_tiles(updated, region, blend_weights)

    other = xor_swap(strip.reshape(-1, NARROW), "z", 1)
    edge = jnp.where(region % 4 == 1, strip[:, -W:], strip[:, :W]).reshape(S * W, NARROW)
    beside = lax.ppermute(
        edge, REGION, [(i, i ^ 3) for i in range(64) if i % 4 in (1, 2)]
    )
    beyond = lax.ppermute(
        edge, REGION, [(i, i ^ 2) for i in range(64) if i % 4 in (1, 2)]
    )
    other, beside, beyond = lax.optimization_barrier((other, beside, beyond))
    edge = jnp.where((region % 4 == 1) | (region % 4 == 2), beside, beyond).reshape(S, W, NARROW)
    joined = join_pair(strip, other.reshape(strip.shape), edge, region, blend_weights)
    return place_tiles(tile_counts, joined.reshape(4, TOK, NARROW))


def solution(mesh):
    fine = Mesh(mesh.devices.reshape(2, 4, 8, 2, 2), REGION + MP)
    return jax.shard_map(
        on_device,
        mesh=fine,
        in_specs=(
            P(REGION, None, MP),
            P(),
            P(REGION, None, None),
            P(REGION, None, MP),
            P(REGION, MP),
            P(),
        ),
        out_specs=P(REGION, None, MP),
        check_vma=False,
    )
```

```python
import functools
import math

import jax
import jax.numpy as jnp
from jax import lax
from jax.experimental import pallas as pl
from jax.experimental.pallas import tpu as pltpu
from jax.sharding import Mesh, PartitionSpec as P

D = 2048
HDIM = 128
S = 16
W = 6
TOK = 256
NARROW = 512
HALF = 256
REGION = ("h", "x", "z")
MP = ("yl", "c")
BF = jnp.bfloat16
F32 = jnp.float32


def xor_swap(block, axis, bit):
    size = math.prod(lax.axis_size(a) for a in ((axis,) if isinstance(axis, str) else axis))
    return lax.ppermute(block, axis, [(i, i ^ bit) for i in range(size)])


def rotate(block, axis, step):
    size = lax.axis_size(axis)
    return lax.ppermute(block, axis, [(i, (i + step) % size) for i in range(size)])


def trade(block, distance, lower):
    route = []
    for i in range(64):
        j = i + distance if lower(i) else i - distance
        if 0 <= j < 64:
            route.append((i, j))
    return lax.ppermute(block, REGION, route)


def opposite(near, side, axis, split_axis):
    size = near.shape[split_axis]
    first = xor_swap(lax.slice_in_dim(side, 0, size // 2, axis=split_axis), axis, 1)
    second = xor_swap(lax.slice_in_dim(near, size // 2, size, axis=split_axis), axis, 3)
    return jnp.concatenate([first, second], axis=split_axis)


def ring_of_four(block, axis, split_axis):
    near = xor_swap(block, axis, 1)
    side = xor_swap(block, axis, 3)
    return block, near, opposite(near, side, axis, split_axis), side


def where_am_i():
    h, x, z = (lax.axis_index(a) for a in REGION)
    yl, c = (lax.axis_index(a) for a in MP)
    return h, x, z, yl, c


def even_count(counts_ref):
    h, x, z, _, _ = where_am_i()
    return counts_ref[h * 32 + x * 8 + (z // 2) * 2]


SMEM = pl.BlockSpec(memory_space=pltpu.SMEM)
VMEM = pl.BlockSpec(memory_space=pltpu.VMEM)
HBM = pl.BlockSpec(memory_space=pltpu.HBM)


def cost(flops, size, special=0):
    return pl.CostEstimate(flops=flops, bytes_accessed=size, transcendentals=special)


def pack_kernel(qkv_ref, out_ref, own, sent):
    h = lax.axis_index("h")
    mine = pl.ds(pl.multiple_of(h * HALF, HALF), HALF)
    theirs = pl.ds(pl.multiple_of((1 - h) * HALF, HALF), HALF)
    for n in range(3):
        own[n] = qkv_ref[n, :, mine]
        sent[n] = qkv_ref[n, :, theirs]
    for n in range(2):
        own[3 + n] = out_ref[:, n * HALF : (n + 1) * HALF]
        sent[3 + n] = out_ref[:, n * HALF : (n + 1) * HALF]


def packed(qkv, out):
    return pl.pallas_call(
        pack_kernel,
        in_specs=[VMEM] * 2,
        out_specs=[VMEM] * 2,
        out_shape=[jax.ShapeDtypeStruct((5, 32, HALF), BF)] * 2,
        cost_estimate=cost(0, 2**18),
        compiler_params=pltpu.CompilerParams(vmem_limit_bytes=8 * 2**20),
        name="pack",
    )(qkv, out)


def split_kernel(counts_ref, data_ref, sent_ref, kept_ref, sem):
    even = even_count(counts_ref)
    odd = lax.axis_index("z") % 2 == 1
    copies = []
    for s in range(2):
        away = jnp.where(odd, jnp.clip(s - even, 0, 3), 2 + s)
        stays = jnp.where(odd, jnp.clip(2 + s - even, 0, 3), s)
        copies.append(pltpu.make_async_copy(data_ref.at[away], sent_ref.at[s], sem))
        copies.append(pltpu.make_async_copy(data_ref.at[stays], kept_ref.at[s], sem))
    for copy in copies:
        copy.start()
    for copy in copies:
        copy.wait()


def split_tiles(counts, data):
    return pl.pallas_call(
        split_kernel,
        in_specs=[SMEM, HBM],
        out_specs=[VMEM, VMEM],
        out_shape=[jax.ShapeDtypeStruct((2, TOK, NARROW), BF)] * 2,
        scratch_shapes=[pltpu.SemaphoreType.DMA],
        cost_estimate=cost(0, 2**21),
        compiler_params=pltpu.CompilerParams(vmem_limit_bytes=12 * 2**20),
        name="split",
    )(counts, data)


def choose_kernel(counts_ref, kept, came, mod, other_mod, tiles, mods, gate):
    even = even_count(counts_ref)
    odd = lax.axis_index("z") % 2 == 1
    place = lax.axis_index("yl") * 2 + lax.axis_index("c")
    cols = pl.ds(pl.multiple_of(place * NARROW, NARROW), NARROW)
    for s in range(2):
        use_other = jnp.where(odd, 2 + s < even, s >= even)

        @pl.when(use_other)
        def _():
            tiles[s] = came[s]
            mods[s] = other_mod[0]
            gate[s] = other_mod[0, 2:3, cols].astype(F32)

        @pl.when(jnp.logical_not(use_other))
        def _():
            tiles[s] = kept[s]
            mods[s] = mod[0]
            gate[s] = mod[0, 2:3, cols].astype(F32)


def choose(counts, kept, came, mod, other_mod):
    return pl.pallas_call(
        choose_kernel,
        in_specs=[SMEM] + [VMEM] * 4,
        out_specs=[VMEM] * 3,
        out_shape=[
            jax.ShapeDtypeStruct((2, TOK, NARROW), BF),
            jax.ShapeDtypeStruct((2, 3, D), BF),
            jax.ShapeDtypeStruct((2, 1, NARROW), F32),
        ],
        cost_estimate=cost(0, 2**21),
        compiler_params=pltpu.CompilerParams(vmem_limit_bytes=12 * 2**20),
        name="choose",
    )(counts, kept, came, mod, other_mod)


def hidden_kernel(a_ref, b_ref, c_ref, d_ref, mod_ref, out_ref):
    place = lax.axis_index("yl") * 2 + lax.axis_index("c")
    parts = [r[...].astype(F32) for r in (a_ref, b_ref, c_ref, d_ref)]
    mean = sum(jnp.sum(p, axis=-1, keepdims=True) for p in parts) * (1.0 / D)
    parts = [p - mean for p in parts]
    spread = sum(jnp.sum(p * p, axis=-1, keepdims=True) for p in parts) * (1.0 / D)
    scale = lax.rsqrt(spread + 1e-06)
    for j, p in enumerate(parts):
        source = pl.ds(pl.multiple_of((place ^ j) * NARROW, NARROW), NARROW)
        gain = 1.0 + mod_ref[0, 1:2, source].astype(F32)
        value = p * scale * gain + mod_ref[0, 0:1, source].astype(F32)
        out_ref[:, j * NARROW : (j + 1) * NARROW] = value.astype(BF)


def hidden_of(pieces, mods):
    rows = 256
    piece = pl.BlockSpec((rows, NARROW), lambda i: (i, 0))
    return pl.pallas_call(
        hidden_kernel,
        grid=(512 // rows,),
        in_specs=[piece] * 4 + [pl.BlockSpec((1, 3, D), lambda i: (i * rows // TOK, 0, 0))],
        out_specs=pl.BlockSpec((rows, D), lambda i: (i, 0)),
        out_shape=jax.ShapeDtypeStruct((512, D), BF),
        cost_estimate=cost(8 * 512 * D, 4 * 512 * D, 512),
        compiler_params=pltpu.CompilerParams(vmem_limit_bytes=24 * 2**20),
        name="hidden",
    )(*pieces, mods)


def attend_kernel(hid_hbm, g_ref, out_ref, hid_ref, w_ref, total_ref, sem):
    h, x, _, yl, c = where_am_i()
    copies = []
    for j in range(4):
        cols = pl.ds(j * NARROW, NARROW)
        group = [pltpu.make_async_copy(hid_hbm.at[:, cols], hid_ref.at[:, cols], sem.at[j])]
        hr = (yl ^ (j // 2)) ^ h
        for half in range(2):
            xr = ((c ^ (j % 2)) * 2 + half) ^ x
            for n in range(3):
                group.append(
                    pltpu.make_async_copy(
                        g_ref.at[:, (xr * 2 + hr) * 3 + n],
                        w_ref.at[j, half, :, :, pl.ds(n * HALF, HALF)],
                        sem.at[j],
                    )
                )
        for copy in group:
            copy.start()
        copies.append(group)
    for j, group in enumerate(copies):
        for copy in group:
            copy.wait()
        part = jnp.dot(
            hid_ref[:, j * NARROW : (j + 1) * NARROW],
            w_ref[j].reshape(NARROW, 3 * HALF),
            preferred_element_type=F32,
        )
        if j == 0:
            total_ref[...] = part
        elif j < 3:
            total_ref[...] += part
    proj = (total_ref[...] + part).astype(BF)

    def block(t, kind, n):
        start = kind * HALF + n * HDIM
        return proj[t * TOK : (t + 1) * TOK, start : start + HDIM]

    units = [(t, n) for t in range(2) for n in range(2)]
    scores = [
        lax.dot_general(
            block(t, 0, n), block(t, 1, n), (((1,), (1,)), ((), ())), preferred_element_type=F32
        )
        * (1.0 / math.sqrt(HDIM))
        for t, n in units
    ]
    exps = [jnp.exp(s - jnp.max(s, axis=-1, keepdims=True)) for s in scores]
    for e, (t, n) in zip(exps, units):
        got = jnp.dot(e.astype(BF), block(t, 2, n), preferred_element_type=F32)
        got = got / jnp.sum(e, axis=-1, keepdims=True)
        out_ref[t * TOK : (t + 1) * TOK, n * HDIM : (n + 1) * HDIM] = got.astype(BF)


def attended_of(hidden, gathered):
    return pl.pallas_call(
        attend_kernel,
        in_specs=[HBM] * 2,
        out_specs=VMEM,
        out_shape=jax.ShapeDtypeStruct((512, HALF), BF),
        scratch_shapes=[
            pltpu.VMEM((512, D), BF),
            pltpu.VMEM((4, 2, 8, 32, 3 * HALF), BF),
            pltpu.VMEM((512, 3 * HALF), F32),
            pltpu.SemaphoreType.DMA((4,)),
        ],
        compiler_params=pltpu.CompilerParams(vmem_limit_bytes=60 * 2**20),
        cost_estimate=cost(
            2 * (2 * 512 * D * 768 + 4 * 4 * TOK * TOK * HDIM), 6 * 2**20, 4 * TOK * TOK
        ),
        name="attend",
    )(hidden, gathered)


def project_kernel(a_ref, b_ref, c_ref, d_ref, o0, o1, o2, o3, keep_ref, send_ref, w_ref, sem):
    h, x, _, _, c = where_am_i()
    copies = []
    for xr, piece in enumerate((o0, o1, o2, o3)):
        px = x ^ xr
        slot = ((px // 2) ^ c) * 2 + px % 2
        for j in range(4):
            block = (j % 2) * 2 + (h ^ (j // 2))
            copies.append(
                pltpu.make_async_copy(
                    piece.at[:, block], w_ref.at[slot, :, :, pl.ds(j * HALF, HALF)], sem
                )
            )
    for copy in copies:
        copy.start()
    for copy in copies:
        copy.wait()
    attended = jnp.concatenate([r[...] for r in (a_ref, b_ref, c_ref, d_ref)], axis=1)
    for b, out_ref in ((1, send_ref), (0, keep_ref)):
        weight = w_ref[2 * b : 2 * b + 2].reshape(NARROW, 4 * HALF)
        total = lax.dot_general(
            attended, weight, (((1,), (1,)), ((), ())), preferred_element_type=F32
        )
        out_ref[...] = total.astype(out_ref.dtype)


def partial_of(attended, os):
    return pl.pallas_call(
        project_kernel,
        in_specs=[VMEM] * 4 + [HBM] * 4,
        out_specs=[VMEM] * 2,
        out_shape=[
            jax.ShapeDtypeStruct((512, NARROW), F32),
            jax.ShapeDtypeStruct((512, NARROW), BF),
        ],
        scratch_shapes=[pltpu.VMEM((4, 8, 32, 4 * HALF), BF), pltpu.SemaphoreType.DMA],
        compiler_params=pltpu.CompilerParams(vmem_limit_bytes=16 * 2**20),
        cost_estimate=cost(2 * 512 * 1024 * 1024, 4 * 2**20),
        name="project",
    )(*attended, *os)


def place_kernel(counts_ref, tiles_ref, out_ref, zero_ref, sem):
    even = even_count(counts_ref)
    parity = lax.axis_index("z") % 2
    zero_ref[...] = jnp.zeros_like(zero_ref)
    waits = []
    for slot in range(4):
        tile = slot + parity * even
        live = jnp.where(parity == 1, tile < 4, slot < even)
        target = out_ref.at[slot]

        @pl.when(live)
        def _():
            pltpu.make_async_copy(tiles_ref.at[jnp.minimum(tile, 3)], target, sem).start()

        @pl.when(jnp.logical_not(live))
        def _():
            pltpu.make_async_copy(zero_ref, target, sem).start()

        waits.append(pltpu.make_async_copy(zero_ref, target, sem))
    for wait in waits:
        wait.wait()


def place_tiles(counts, tiles):
    return pl.pallas_call(
        place_kernel,
        in_specs=[SMEM, VMEM],
        out_specs=HBM,
        out_shape=jax.ShapeDtypeStruct((4, TOK, NARROW), BF),
        scratch_shapes=[pltpu.VMEM((TOK, NARROW), BF), pltpu.SemaphoreType.DMA],
        cost_estimate=cost(0, 2**21),
        compiler_params=pltpu.CompilerParams(vmem_limit_bytes=12 * 2**20),
        name="place",
    )(counts, tiles)


def mix(earlier, later, share):
    return ((1.0 - share) * earlier.astype(F32) + share * later.astype(F32)).astype(BF)


def join_rows(strip, region, shares):
    count = strip.shape[1]
    share = shares.reshape(W, 1, 1)
    top, bottom = strip[:W], strip[S - W :]
    north, south = top.reshape(W * count, NARROW), bottom.reshape(W * count, NARROW)
    first = region % 8 < 4
    cross = trade(jnp.where(first, north, south), 4, lambda i: i % 8 >= 4)
    same = trade(jnp.where(first, south, north), 4, lambda i: i % 8 < 4)
    cross, same = lax.optimization_barrier((cross, same))
    later, earlier = jnp.where(first, same, cross), jnp.where(first, cross, same)
    top = jnp.where(region >= 4, mix(earlier.reshape(W, count, NARROW), top, share), top)
    bottom = jnp.where(region < 60, mix(bottom, later.reshape(W, count, NARROW), share), bottom)
    return jnp.concatenate([top, strip[W : S - W], bottom], axis=0)


def join_tiles(tiles, region, shares):
    first, second = tiles[0], tiles[1]
    inner = mix(first[:, S - W :], second[:, :W], shares.reshape(1, W, 1))
    strip = jnp.concatenate([first[:, : S - W], inner, second[:, W:]], axis=1)
    return join_rows(strip, region, shares)


def join_pair(own, other, edge, region, shares):
    share = shares.reshape(1, W, 1)
    odd = region % 2 == 1
    low, high = jnp.where(odd, other, own), jnp.where(odd, own, other)
    west, east = low[:, :W], high[:, -W:]
    front = region % 4 < 2
    west = jnp.where(front, west, mix(edge, west, share))
    east = jnp.where(front, mix(east, edge, share), east)
    middle = mix(low[:, -W:], high[:, :W], share)
    n = 2 * S - W
    return jnp.stack(
        [
            jnp.concatenate([west, low[:, W:S]], axis=1),
            jnp.concatenate([low[:, S - W : n - W], middle], axis=1),
            jnp.concatenate([middle, high[:, W:S]], axis=1),
            jnp.concatenate([high[:, S - W : n - W], east], axis=1),
        ]
    )


def on_device(tile_data, tile_counts, modulation, qkv_weight, out_weight, blend_weights):
    h, x, z, yl, _ = where_am_i()
    region = h * 32 + x * 8 + z
    ring = ("h", "yl")

    own_blocks, sent_blocks = packed(qkv_weight.transpose(1, 0, 2), out_weight)
    came_blocks = xor_swap(sent_blocks, "h", 1)

    tile_data, sent_blocks = lax.optimization_barrier((tile_data, sent_blocks))
    away, kept = split_tiles(tile_counts, tile_data)
    came = xor_swap(away, "z", 1)
    came_mod = xor_swap(modulation, "z", 1)

    came_blocks, kept = lax.optimization_barrier((came_blocks, kept))
    straight = yl == h
    out_kept = jnp.where(straight, own_blocks[3:], came_blocks[3:])
    out_sent = jnp.where(straight, came_blocks[3:], own_blocks[3:])
    qkv = jnp.concatenate([own_blocks[:3], came_blocks[:3]])
    qkv, out_sent = lax.optimization_barrier((qkv, out_sent))
    x_far, x_near, x_side = (xor_swap(qkv, "x", bit) for bit in (2, 1, 3))
    out_came = xor_swap(out_sent, "yl", 1)
    x_far, x_near, x_side, out_came = lax.optimization_barrier((x_far, x_near, x_side, out_came))
    block = jnp.concatenate([qkv, x_near, x_far, x_side, out_kept, out_came])
    gathered = lax.all_gather(block, "z", axis=0)

    tiles, mods, gate = choose(tile_counts, kept, came, modulation, came_mod)
    mine = tiles.reshape(512, NARROW)
    _, near, across, side = ring_of_four(mine, ring, 0)
    mods_across = xor_swap(mods, "h", 1)
    hid_own = hidden_of((mine, xor_swap(mine, "c", 1), near, xor_swap(near, "c", 1)), mods)
    across, hid_own, mods_across = lax.optimization_barrier((across, hid_own, mods_across))
    hid_other = hidden_of(
        (across, xor_swap(across, "c", 1), side, xor_swap(side, "c", 1)), mods_across
    )
    hid_own, hid_other = lax.optimization_barrier((hid_own, hid_other))

    att_sent = attended_of(hid_other, gathered)
    o_block = gathered[:, 24:]
    hid_own, att_sent = lax.optimization_barrier((hid_own, att_sent))
    o_near, o_side = xor_swap(o_block, "x", 1), xor_swap(o_block, "x", 3)
    att_side, att_relay = xor_swap(att_sent, ring, 3), xor_swap(att_sent, ring, 1)
    att_own = attended_of(hid_own, gathered)
    o_near, o_side, att_relay, att_side, att_own = lax.optimization_barrier(
        (o_near, o_side, att_relay, att_side, att_own)
    )
    att_near, att_across = xor_swap(att_own, ring, 1), xor_swap(att_relay, ring, 3)
    o_all = (o_block, o_near, opposite(o_near, o_side, "x", 0), o_side)

    keep, send = partial_of((att_own, att_near, att_across, att_side), o_all)
    summed = keep + xor_swap(send, "c", 1).astype(F32)
    updated = tiles.astype(F32) + gate * summed.reshape(2, TOK, NARROW)
    updated = updated.astype(BF).reshape(2, S, S, NARROW)
    strip = join_tiles(updated, region, blend_weights)

    other = xor_swap(strip.reshape(-1, NARROW), "z", 1)
    edge = jnp.where(region % 4 == 1, strip[:, -W:], strip[:, :W]).reshape(S * W, NARROW)
    beside = lax.ppermute(
        edge, REGION, [(i, i ^ 3) for i in range(64) if i % 4 in (1, 2)]
    )
    beyond = lax.ppermute(
        edge, REGION, [(i, i ^ 2) for i in range(64) if i % 4 in (1, 2)]
    )
    other, beside, beyond = lax.optimization_barrier((other, beside, beyond))
    edge = jnp.where((region % 4 == 1) | (region % 4 == 2), beside, beyond).reshape(S, W, NARROW)
    joined = join_pair(strip, other.reshape(strip.shape), edge, region, blend_weights)
    return place_tiles(tile_counts, joined.reshape(4, TOK, NARROW))


def solution(mesh):
    fine = Mesh(mesh.devices.reshape(2, 4, 8, 2, 2), REGION + MP)
    return jax.shard_map(
        on_device,
        mesh=fine,
        in_specs=(
            P(REGION, None, MP),
            P(),
            P(REGION, None, None),
            P(REGION, None, MP),
            P(REGION, MP),
            P(),
        ),
        out_specs=P(REGION, None, MP),
        check_vma=False,
    )
```
